512 devices in a mesh: slab: 64 (over z, y), pencil: 8 (over x, core).
Axes of the slice: x: 4, y: 4, z: 16, core: 2. Of those that a mesh axis runs over, the one named last changes fastest.
Arguments:
- cells: int32 [512, 5632], P(('slab', 'pencil')), may hold values from 0 to 32767
- fractions: float32 [3, 512, 5632], P(None, ('slab', 'pencil')), may hold values from 0 to 1
- adjoint_pos: float32 [3, 512, 5632], P(None, ('slab', 'pencil')), may hold values from -6 to 6
- adjoint_vel: float32 [3, 512, 5632], P(None, ('slab', 'pencil')), may hold values from -6 to 6
- counts: int32 [512, 521], P(('slab', 'pencil')), may hold values from 0 to 512, as said below
Outputs:
- mode_grad: float32 [2, 256, 256, 256], P(None, 'slab', 'pencil')
The draws below stay inside these ranges and needn't reach their ends.
Inputs may be any that keep to these rules, and one draw needn't show every extreme that they name: Live slots come first in each group; slots at or past the count hold unused values. Near counts are at most 512 and tail counts at most 2. In every draw some owner receives 512 live slots in every near group aimed at it, and some tail count equals 2.
All inputs are finite; a program needn't handle non-finite values.
Results may differ from the reference program's by a relative error of at most 0.004.
Values sent between devices are 32-bit elements; how exact they have to be, the bound alone decides.
No kernel may reach another device: no remote copies, remote signals or barrier semaphores. Data moves between devices by JAX's collectives and lax.ppermute only.
A program may use at most 64 MiB of HBM per device.

```python
import jax
import jax.numpy as jnp

NG = 256
CAP = 512
TAIL = 2
OWNERS = 512
SLOTS = 5632
CX = 4
CY = 32
N_SLAB = 64
N_PENCIL = 8


def draw_counts(key, part):
    key = jax.random.fold_in(key, 11)
    pick_key, near_key, tail_key, extra_key = jax.random.split(key, 4)
    full_owner = jax.random.randint(pick_key, (), 0, OWNERS)
    group = jnp.arange(9)
    holder = jnp.arange(OWNERS)[:, None]
    slab_count = OWNERS // N_PENCIL
    near_owner = (holder // N_PENCIL + group[None, :] // 3 - 1) % slab_count * N_PENCIL + (holder % N_PENCIL + group[None, :] % 3 - 1) % N_PENCIL
    near = jax.random.randint(near_key, (OWNERS, 9), CAP // 2, CAP + 1)
    near = jnp.where(near_owner == full_owner, CAP, near)
    tail_pick = jax.random.randint(tail_key, (OWNERS, OWNERS), 0, 4)
    tail = jnp.where(tail_pick == 0, TAIL, 0)
    extra_holder = jax.random.randint(extra_key, (), 0, OWNERS)
    owner_ids = jnp.arange(OWNERS)[None, :]
    tail = jnp.where((holder == extra_holder) & (owner_ids == full_owner), TAIL, tail)
    return jnp.concatenate([near, tail], axis=1).astype(jnp.int32)


def place_ends(values, stream_key, smallest, high):
    longest = values.shape.index(max(values.shape))
    spots = []
    for shift in (0, 1):
        where = [jax.random.randint(jax.random.fold_in(stream_key, axis), (), 0, length) for axis, length in enumerate(values.shape)]
        where[longest] = (where[longest] + shift) % values.shape[longest]
        spots.append(tuple(where))
    return values.at[spots[0]].set(smallest).at[spots[1]].set(high)


def block_levels(stream_key, dims, cuts, low, largest):
    gain, own = 1.0, jax.random.fold_in(stream_key, 6)
    for dim, blocks in cuts:
        heights = jnp.exp(jax.random.uniform(jax.random.fold_in(own, dim), (blocks,), jnp.float32, low / len(cuts), largest / len(cuts)))
        gain = gain * jnp.repeat(heights, dims[dim] // blocks).reshape([-1 if axis == dim else 1 for axis in range(len(dims))])
    return gain


def centred(own_key, dims, width, reach, pieces=(), kind=jnp.bfloat16):
    entries = width * jax.random.normal(own_key, dims, jnp.float32)
    if pieces:
        entries = entries * block_levels(own_key, dims, pieces, -0.22, 0.18)
    return jnp.clip(entries, -reach, reach).astype(kind)


def setup_inputs(seed: int = 0) -> dict:
    key_of = jax.random.split(jax.random.key(seed), 6)
    cells = place_ends(jax.random.randint(key_of[0], (OWNERS, SLOTS), 0, CX * CY * NG), jax.random.fold_in(key_of[0], 1), 0, (CX * CY * NG) - 1).astype(jnp.int32)
    fractions = jnp.clip(1.0 * jax.random.uniform(key_of[1], (3, OWNERS, SLOTS), jnp.float32) ** block_levels(key_of[1], (3, OWNERS, SLOTS), ((1, 512),), -0.2, 0.2), 0.0, 1.0)
    adjoint_pos = centred(key_of[2], (3, OWNERS, SLOTS), 1.0, 6.0, ((1, 512),), jnp.float32)
    adjoint_vel = centred(key_of[3], (3, OWNERS, SLOTS), 1.0, 6.0, ((1, 512),), jnp.float32)
    counts = draw_counts(jax.random.fold_in(key_of[5], 71), 0)
    return dict(cells=cells, fractions=fractions, adjoint_pos=adjoint_pos, adjoint_vel=adjoint_vel, counts=counts)


kick_factor = 0.8
drift_factor = 1.25
out_scale = 3.0

def wavenumber(position, length):
    return jnp.where(position < length // 2, position, position - length).astype(jnp.float32)

def reference(cells, fractions, adjoint_pos, adjoint_vel, counts):
    owners = counts.shape[0]
    group = jnp.arange(9, dtype=jnp.int32)
    holder = jnp.arange(owners, dtype=jnp.int32)[:, None]
    holder_slab = holder // N_PENCIL
    holder_pencil = holder % N_PENCIL
    near_owner = (holder_slab + group[None, :] // 3 - 1) % N_SLAB * N_PENCIL + (holder_pencil + group[None, :] % 3 - 1) % N_PENCIL
    near_slots = jnp.repeat(near_owner, CAP, axis=1)
    tail_slots = jnp.broadcast_to(jnp.repeat(jnp.arange(owners, dtype=jnp.int32), TAIL)[None, :], (owners, owners * TAIL))
    slot_owner = jnp.concatenate([near_slots, tail_slots], axis=1).astype(jnp.int32)
    near_live = (jnp.arange(CAP, dtype=jnp.int32)[None, None, :] < counts[:, :9, None]).reshape(owners, 9 * CAP)
    tail_live = (jnp.arange(TAIL, dtype=jnp.int32)[None, None, :] < counts[:, 9:, None]).reshape(owners, owners * TAIL)
    live_mask = jnp.concatenate([near_live, tail_live], axis=1).astype(jnp.float32)
    weight = kick_factor * (adjoint_vel + drift_factor * adjoint_pos) * live_mask[None]
    base_x = slot_owner // N_PENCIL * CX + cells // (CY * NG)
    base_y = slot_owner % N_PENCIL * CY + cells // NG % CY
    base_z = cells % NG
    frac_x = fractions[0]
    frac_y = fractions[1]
    frac_z = fractions[2]
    low_part = (weight * (1.0 - frac_z)[None]).astype(jnp.bfloat16).astype(jnp.float32)
    high_part = (weight * frac_z[None]).astype(jnp.bfloat16).astype(jnp.float32)
    painted = jnp.zeros((3, NG * NG * NG), jnp.float32)
    for step_x in (0, 1):
        weight_x = frac_x if step_x else 1.0 - frac_x
        for step_y in (0, 1):
            weight_y = frac_y if step_y else 1.0 - frac_y
            corner = (weight_x * weight_y).astype(jnp.bfloat16).astype(jnp.float32)
            for step_z, z_line in ((0, low_part), (1, high_part)):
                target = ((base_x + step_x) % NG * NG + (base_y + step_y) % NG) * NG + (base_z + step_z) % NG
                painted = painted.at[:, target.reshape(-1)].add((corner[None] * z_line).reshape(3, -1))
    mesh_field = painted.reshape(3, NG, NG, NG)
    spectrum = jnp.fft.fftn(mesh_field, axes=(1, 2, 3))
    wave = wavenumber(jnp.arange(NG, dtype=jnp.int32), NG)
    mixed = wave[:, None, None] * spectrum[0] + wave[None, :, None] * spectrum[1] + wave[None, None, :] * spectrum[2]
    wave_sq = wave[:, None, None] ** 2 + wave[None, :, None] ** 2 + wave[None, None, :] ** 2
    factor = jnp.where(wave_sq > 0, out_scale / jnp.sqrt(jnp.maximum(wave_sq, 1.0)), 0.0) / NG ** 1.5
    result = jnp.stack([jnp.imag(mixed) * factor, -jnp.real(mixed) * factor]).astype(jnp.float32)
    return jnp.transpose(result, (0, 2, 3, 1))
```

```python
import functools

import jax
import jax.numpy as jnp
import ml_dtypes
import numpy as np
from jax import lax
from jax.experimental import pallas as pl
from jax.experimental.pallas import tpu as pltpu
from jax.sharding import PartitionSpec as P

NG = 256
CAP = 512
TAIL = 2
N_SLAB = 64
N_PENCIL = 8
OWNERS = 512
NEAR = 9 * CAP
TAILS = OWNERS * TAIL
CX = 4
CY = 32
STRIDE = 40
MAIN = CX * STRIDE
PAINT_ROWS = MAIN + STRIDE
CHUNK = 6 * CY + 8

kick_factor = 0.8
drift_factor = 1.25
out_scale = 3.0

f32 = jnp.float32
bf16 = jnp.bfloat16
VMEM = pl.BlockSpec(memory_space=pltpu.VMEM)
SMEM = pl.BlockSpec(memory_space=pltpu.SMEM)
PARAMS = pltpu.CompilerParams(vmem_limit_bytes=24 * 1024 * 1024)


def split_table(table):
    high = table.astype(ml_dtypes.bfloat16)
    low = (table - high.astype(np.float64)).astype(ml_dtypes.bfloat16)
    return high, low


@functools.cache
def host_tables():
    idx = np.arange(NG)
    angles = (idx[:, None] * idx[None, :] % NG) * (2.0 * np.pi / NG)
    cosine, sine = np.cos(angles), np.sin(angles)
    wave = np.where(idx < NG // 2, idx, idx - NG).astype(np.float64)
    table_z = np.concatenate([cosine, -sine], axis=1)
    table_kz = np.concatenate([cosine * wave[None, :], -sine * wave[None, :]], axis=1)
    table_k = np.concatenate([cosine * wave[:, None], sine * wave[:, None], cosine, sine], axis=1)
    order = np.array([4 * s + r for r in range(4) for s in range(N_SLAB)])
    return (
        split_table(table_z),
        split_table(table_kz),
        split_table(table_k[order]),
        split_table(table_k),
    )


def shifted(block, axis, distance):
    devices = range(lax.axis_size(axis))
    route = [((i - distance) % len(devices), i) for i in devices]
    return lax.ppermute(block, axis, route)


def product(table_high, table_low, data):
    high = data.astype(bf16)
    low = (data - high.astype(f32)).astype(bf16)
    dot = functools.partial(jnp.dot, preferred_element_type=f32)
    return dot(table_high, high) + (dot(table_high, low) + dot(table_low, high))


def pack_kernel(counts_ref, counts_vec_ref, cells_ref, frac_ref, pos_ref, vel_ref, down_ref, mid_ref, up_ref, tail_ref, rows, columns):
    for group in range(9):
        out = (down_ref, mid_ref, up_ref)[group // 3]
        src = pl.ds(group * CAP, CAP)
        dst = pl.ds(group % 3 * CAP, CAP)
        live = lax.broadcasted_iota(jnp.int32, (1, CAP), 1) < counts_ref[0, group]
        out[0:1, dst] = cells_ref[:, src].astype(f32)
        for i in range(3):
            out[1 + i : 2 + i, dst] = frac_ref[i, :, src]
            weight = kick_factor * (vel_ref[i, :, src] + drift_factor * pos_ref[i, :, src])
            out[4 + i : 5 + i, dst] = jnp.where(live, weight, 0.0)
        out[7:8, dst] = jnp.zeros((1, CAP), f32)
    width = counts_vec_ref.shape[1]
    slot_of = lax.broadcasted_iota(jnp.int32, (width, TAILS), 1)
    entry = lax.broadcasted_iota(jnp.int32, (width, TAILS), 0)
    spread = jnp.where(slot_of // TAIL + 9 == entry, 1.0, 0.0).astype(bf16)
    counts = jnp.broadcast_to(counts_vec_ref[...].astype(f32), (8, width)).astype(bf16)
    tail_count = jnp.dot(counts, spread, preferred_element_type=f32)[0:1]
    live = (lax.broadcasted_iota(jnp.int32, (1, TAILS), 1) % TAIL).astype(f32) < tail_count
    src = pl.ds(NEAR, TAILS)
    rows[0:1] = cells_ref[:, src].astype(f32)
    for i in range(3):
        rows[1 + i : 2 + i] = frac_ref[i, :, src]
        weight = kick_factor * (vel_ref[i, :, src] + drift_factor * pos_ref[i, :, src])
        rows[4 + i : 5 + i] = jnp.where(live, weight, 0.0)
    rows[7:8] = jnp.zeros((1, TAILS), f32)
    columns[...] = rows[...].T
    for k in range(16):
        tail_ref[:, 8 * k : 8 * k + 8] = columns[pl.ds(k, N_SLAB, stride=16), :]


def pack(counts, cells, fractions, adjoint_pos, adjoint_vel):
    side = jax.ShapeDtypeStruct((8, 3 * CAP), f32)
    return pl.pallas_call(
        pack_kernel,
        out_shape=(side, side, side, jax.ShapeDtypeStruct((N_SLAB, 128), f32)),
        in_specs=[SMEM] + [VMEM] * 5,
        out_specs=(VMEM,) * 4,
        scratch_shapes=[pltpu.VMEM((8, TAILS), f32), pltpu.VMEM((TAILS, 8), f32)],
        compiler_params=PARAMS,
        name="pack",
    )(counts, counts, cells, fractions, adjoint_pos, adjoint_vel)


def repack_kernel(in_ref, out_ref):
    for p in range(N_PENCIL):
        for k in range(8):
            out_ref[p, :, 16 * k : 16 * k + 16] = in_ref[8 * k : 8 * k + 8, 16 * p : 16 * p + 16]


def repack(tail):
    return pl.pallas_call(
        repack_kernel,
        out_shape=jax.ShapeDtypeStruct((N_PENCIL, 8, 128), f32),
        in_specs=[VMEM],
        out_specs=VMEM,
        compiler_params=PARAMS,
        name="repack",
    )(tail)


def paint(values, acc_ref):
    slots = values.shape[1]
    cell = values[0:1].astype(jnp.int32)
    row = lax.shift_right_logical(cell, 13) * STRIDE + (lax.shift_right_logical(cell, 8) & 31)
    base_z = cell & 255
    next_z = (base_z + 1) & 255
    frac_x, frac_y, frac_z = values[1:2], values[2:3], values[3:4]
    rest_x, rest_y, rest_z = 1.0 - frac_x, 1.0 - frac_y, 1.0 - frac_z

    def rounded(value):
        return value.astype(bf16).astype(f32)

    row_ids = lax.broadcasted_iota(jnp.int32, (PAINT_ROWS, slots), 0)
    corner = jnp.where(row_ids == row, rounded(rest_x * rest_y), 0.0)
    corner = jnp.where(row_ids == row + 1, rounded(rest_x * frac_y), corner)
    corner = jnp.where(row_ids == row + STRIDE, rounded(frac_x * rest_y), corner)
    corner = jnp.where(row_ids == row + STRIDE + 1, rounded(frac_x * frac_y), corner).astype(bf16)
    z_ids = lax.broadcasted_iota(jnp.int32, (NG, slots), 0)
    at_low, at_high = z_ids == base_z, z_ids == next_z
    for i in range(3):
        weight = values[4 + i : 5 + i]
        line = jnp.where(at_low, rounded(weight * rest_z), 0.0)
        line = jnp.where(at_high, rounded(weight * frac_z), line).astype(bf16)
        acc_ref[:, i * NG : (i + 1) * NG] += lax.dot_general(
            corner, line, (((1,), (1,)), ((), ())), preferred_element_type=f32
        )


def near_kernel(down_ref, left_ref, mid_ref, right_ref, up_ref, out_ref):
    out_ref[...] = jnp.zeros_like(out_ref)
    for ref in (left_ref, mid_ref, right_ref):
        paint(ref[:, CAP : 2 * CAP], out_ref)

    def body(step, carry):
        at = pl.ds(pl.multiple_of(step * CAP, CAP), CAP)
        paint(down_ref[:, at], out_ref)
        paint(up_ref[:, at], out_ref)
        return carry

    lax.fori_loop(0, 3, body, 0)


def paint_near(down, left, mid, right, up):
    return pl.pallas_call(
        near_kernel,
        out_shape=jax.ShapeDtypeStruct((PAINT_ROWS, 3 * NG), f32),
        in_specs=[VMEM] * 5,
        out_specs=VMEM,
        compiler_params=PARAMS,
        cost_estimate=pl.CostEstimate(flops=2 * NEAR * PAINT_ROWS * 3 * NG, bytes_accessed=2_000_000, transcendentals=0),
        name="paint_near",
    )(down, left, mid, right, up)


def tail_kernel(tail_ref, near_ref, main_ref, spill_ref, values, acc):
    turned = tail_ref[...].T
    for k in range(16):
        values[:, 64 * k : 64 * k + 64] = turned[8 * k : 8 * k + 8, :]
    acc[...] = near_ref[...]
    for half in range(2):
        paint(values[:, half * 512 : half * 512 + 512], acc)
    main_ref[...] = acc[:MAIN]
    spill_ref[...] = acc[MAIN:]


def paint_tail(tail, near):
    return pl.pallas_call(
        tail_kernel,
        out_shape=(jax.ShapeDtypeStruct((MAIN, 3 * NG), f32), jax.ShapeDtypeStruct((STRIDE, 3 * NG), f32)),
        in_specs=[VMEM] * 2,
        out_specs=(VMEM,) * 2,
        scratch_shapes=[pltpu.VMEM((8, TAILS), f32), pltpu.VMEM((PAINT_ROWS, 3 * NG), f32)],
        compiler_params=PARAMS,
        name="paint_tail",
    )(tail, near)


def z_kernel(main_ref, spill_ref, plain_high, plain_low, scaled_high, scaled_low, out_ref):
    for i in range(3):
        columns = pl.ds(i * NG, NG)
        data = jnp.concatenate(
            [main_ref[:STRIDE, columns] + spill_ref[:, columns], main_ref[STRIDE:, columns]], axis=0
        )
        high = data.astype(bf16)
        low = (data - high.astype(f32)).astype(bf16)
        table_high, table_low = (scaled_high, scaled_low) if i == 2 else (plain_high, plain_low)
        dot = functools.partial(jnp.dot, preferred_element_type=f32)
        result = dot(high, table_high[...]) + (dot(low, table_high[...]) + dot(high, table_low[...]))
        for part in range(2):
            block = 2 * i + part
            for p in range(N_PENCIL):
                at = part * NG + p * 32
                chunk = jnp.concatenate(
                    [result[x * STRIDE : (x + 1) * STRIDE, at : at + 32] for x in range(CX)], axis=1
                )
                out_ref[p, block * CY : (block + 1) * CY, :] = chunk[:CY]
                out_ref[p, 6 * CY + block : 6 * CY + block + 1, :] = chunk[CY : CY + 1]
    out_ref[:, 6 * CY + 6 :, :] = jnp.zeros((N_PENCIL, 2, 128), f32)


def transform_z(main, spill, plain, scaled):
    return pl.pallas_call(
        z_kernel,
        out_shape=jax.ShapeDtypeStruct((N_PENCIL, CHUNK, 128), f32),
        in_specs=[VMEM] * 6,
        out_specs=VMEM,
        compiler_params=PARAMS,
        name="transform_z",
    )(main, spill, *plain, *scaled)


def mixed_rhs(real, imag):
    return jnp.concatenate(
        [jnp.concatenate([real, imag], axis=1), jnp.concatenate([imag, -real], axis=1)], axis=0
    )


def y_kernel(in_ref, table_high, table_low, out_ref):
    first = lax.broadcasted_iota(jnp.int32, (CY, 128), 0) == 0
    blocks = []
    for block in range(6):
        parts = []
        for src in range(N_PENCIL):
            spilled = in_ref[(src - 1) % N_PENCIL, 6 * CY + block : 6 * CY + block + 1, :]
            parts.append(in_ref[src, block * CY : (block + 1) * CY, :] + jnp.where(first, spilled, 0.0))
        blocks.append(jnp.concatenate(parts, axis=0))
    field = product(table_high[:, 2 * NG :], table_low[:, 2 * NG :], mixed_rhs(blocks[0], blocks[1]))
    sides = jnp.concatenate([mixed_rhs(blocks[2], blocks[3]), mixed_rhs(blocks[4], blocks[5])], axis=0)
    mixed = product(table_high[...], table_low[...], sides)
    for f, result in enumerate((field, mixed)):
        for part in range(2):
            for x in range(CX):
                at = part * 128 + x * 32
                chunk = jnp.concatenate(
                    [result[r * N_SLAB : (r + 1) * N_SLAB, at : at + 32] for r in range(4)], axis=1
                )
                out_ref[pl.ds(x * 4 + f * 2 + part, N_SLAB, stride=16), :] = chunk


def transform_y(by_rows, table):
    return pl.pallas_call(
        y_kernel,
        out_shape=jax.ShapeDtypeStruct((N_SLAB * 16, 128), f32),
        in_specs=[VMEM] * 3,
        out_specs=VMEM,
        compiler_params=PARAMS,
        name="transform_y",
    )(by_rows, *table)


def wavenumber(position):
    return jnp.where(position < NG // 2, position, position - NG).astype(f32)


def x_kernel(place_ref, in_ref, table_high, table_low, out_ref):
    lines = [in_ref[pl.ds(block, NG, stride=4), :] for block in range(4)]
    data = jnp.concatenate([mixed_rhs(lines[0], lines[1]), mixed_rhs(lines[2], lines[3])], axis=0)
    mixed = product(table_high[...], table_low[...], data)
    lane = lax.broadcasted_iota(jnp.int32, (1, 128), 1)
    wave_y = wavenumber(place_ref[0] * 4 + lane // 32)
    wave_z = wavenumber(place_ref[1] * 32 + lane % 32)
    wave_x = wavenumber(lax.broadcasted_iota(jnp.int32, (NG, 1), 0))
    wave_sq = wave_x * wave_x + wave_y * wave_y + wave_z * wave_z
    factor = jnp.where(wave_sq > 0, out_scale / jnp.sqrt(jnp.maximum(wave_sq, 1.0)), 0.0) / NG**1.5
    out_ref[0] = (mixed[:, 128:] * factor).T
    out_ref[1] = (mixed[:, :128] * -factor).T


def transform_x(place, by_cols, table):
    return pl.pallas_call(
        x_kernel,
        out_shape=jax.ShapeDtypeStruct((2, 128, NG), f32),
        in_specs=[SMEM] + [VMEM] * 3,
        out_specs=VMEM,
        compiler_params=PARAMS,
        name="transform_x",
    )(place, by_cols, *table)


def local(cells, fractions, adjoint_pos, adjoint_vel, counts):
    plain, scaled, table_y, table_x = [tuple(jnp.asarray(t) for t in pair) for pair in host_tables()]
    to_below, own, to_above, tail = pack(counts, cells, fractions, adjoint_pos, adjoint_vel)
    tail = lax.all_to_all(tail.reshape(N_SLAB, 1, 128), "slab", 0, 0, tiled=True)
    from_above = shifted(to_below, "slab", -1)
    from_below = shifted(to_above, "slab", 1)
    tail = repack(tail.reshape(N_SLAB, 128))
    tail = lax.all_to_all(tail, "pencil", 0, 0, tiled=True)
    bands = (from_above, own, from_below)
    to_left = jnp.concatenate([band[:, :CAP] for band in bands], axis=1)
    to_right = jnp.concatenate([band[:, 2 * CAP :] for band in bands], axis=1)
    from_right = shifted(to_left, "pencil", -1)
    from_left = shifted(to_right, "pencil", 1)
    near = paint_near(from_left, from_above, own, from_below, from_right)
    main, spill = paint_tail(tail.reshape(N_SLAB, 128), near)
    spill = shifted(spill, "slab", 1)
    by_rows = transform_z(main, spill, plain, scaled)
    by_rows = lax.all_to_all(by_rows, "pencil", 0, 0, tiled=True)
    by_cols = transform_y(by_rows, table_y)
    by_cols = lax.all_to_all(by_cols.reshape(N_SLAB, 16, 128), "slab", 0, 0, tiled=True)
    place = jnp.stack([lax.axis_index("slab"), lax.axis_index("pencil")]).astype(jnp.int32)
    result = transform_x(place, by_cols.reshape(N_SLAB * 16, 128), table_x)
    return result.reshape(2, CX, 32, NG)


def solution(mesh):
    in_specs = (
        P(("slab", "pencil"), None),
        P(None, ("slab", "pencil"), None),
        P(None, ("slab", "pencil"), None),
        P(None, ("slab", "pencil"), None),
        P(("slab", "pencil"), None),
    )
    out_specs = P(None, "slab", "pencil", None)
    return jax.shard_map(local, mesh=mesh, in_specs=in_specs, out_specs=out_specs, check_vma=False)
```

```python
import functools

import jax
import jax.numpy as jnp
import ml_dtypes
import numpy as np
from jax import lax
from jax.experimental import pallas as pl
from jax.experimental.pallas import tpu as pltpu
from jax.sharding import PartitionSpec as P

NG = 256
CAP = 512
TAIL = 2
N_SLAB = 64
N_PENCIL = 8
OWNERS = 512
NEAR = 9 * CAP
TAILS = OWNERS * TAIL
CX = 4
CY = 32
STRIDE = 40
MAIN = CX * STRIDE
CHUNK = 6 * CY + 8

kick_factor = 0.8
drift_factor = 1.25
out_scale = 3.0

f32 = jnp.float32
bf16 = jnp.bfloat16
VMEM = pl.BlockSpec(memory_space=pltpu.VMEM)
SMEM = pl.BlockSpec(memory_space=pltpu.SMEM)
HBM = pl.BlockSpec(memory_space=pltpu.HBM)
ANY = pl.BlockSpec(memory_space=pl.ANY)
WIDE = pltpu.CompilerParams(vmem_limit_bytes=60 * 1024 * 1024)
PARAMS = pltpu.CompilerParams(vmem_limit_bytes=24 * 1024 * 1024)


def split_table(table):
    high = table.astype(ml_dtypes.bfloat16)
    low = (table - high.astype(np.float64)).astype(ml_dtypes.bfloat16)
    return high, low


@functools.cache
def host_tables():
    idx = np.arange(NG)
    angles = (idx[:, None] * idx[None, :] % NG) * (2.0 * np.pi / NG)
    cosine, sine = np.cos(angles), np.sin(angles)
    wave = np.where(idx < NG // 2, idx, idx - NG).astype(np.float64)
    table_z = np.concatenate([cosine, -sine], axis=1)
    table_kz = np.concatenate([cosine * wave[None, :], -sine * wave[None, :]], axis=1)
    table_k = np.concatenate([cosine * wave[:, None], sine * wave[:, None], cosine, sine], axis=1)
    order = np.array([4 * s + r for r in range(4) for s in range(N_SLAB)])
    return (
        split_table(table_z),
        split_table(table_kz),
        split_table(table_k[order]),
        split_table(table_k),
    )


def shifted(block, axis, distance):
    devices = range(lax.axis_size(axis))
    route = [((i - distance) % len(devices), i) for i in devices]
    return lax.ppermute(block, axis, route)


def product(table_high, table_low, data):
    high = data.astype(bf16)
    low = (data - high.astype(f32)).astype(bf16)
    dot = functools.partial(jnp.dot, preferred_element_type=f32)
    return dot(table_high, high) + (dot(table_high, low) + dot(table_low, high))


def start_copies(pairs, sems):
    copies = [pltpu.make_async_copy(src, dst, sems.at[i]) for i, (src, dst) in enumerate(pairs)]
    for copy in copies:
        copy.start()
    return copies


def particle_rows(out, lanes, live, cells, frac, pos, vel):
    out[0:1, lanes] = cells.astype(f32)
    for i in range(3):
        out[1 + i : 2 + i, lanes] = frac[i]
        weight = kick_factor * (vel[i] + drift_factor * pos[i])
        out[4 + i : 5 + i, lanes] = jnp.where(live, weight, 0.0)
    out[7:8, lanes] = jnp.zeros(cells.shape, f32)


def pack_kernel(counts_smem, counts_hbm, cells_hbm, frac_hbm, pos_hbm, vel_hbm, tail_ref, left_ref, mid_ref, right_ref, counts_ref, cells_ref, frac_ref, pos_ref, vel_ref, rows, columns, flat, sems):
    copies = start_copies(
        [(counts_hbm, counts_ref), (cells_hbm, cells_ref), (frac_hbm, frac_ref), (pos_hbm, pos_ref), (vel_hbm, vel_ref)], sems
    )
    width = counts_ref.shape[1]
    slot_of = lax.broadcasted_iota(jnp.int32, (width, TAILS), 1)
    entry = lax.broadcasted_iota(jnp.int32, (width, TAILS), 0)
    spread = jnp.where(slot_of // TAIL + 9 == entry, 1.0, 0.0).astype(bf16)
    for copy in copies:
        copy.wait()

    def fill(out, lanes, src, live):
        particle_rows(out, lanes, live, cells_ref[:, src], frac_ref[:, :, src], pos_ref[:, :, src], vel_ref[:, :, src])

    counts = jnp.broadcast_to(counts_ref[...].astype(f32), (8, width)).astype(bf16)
    tail_count = jnp.dot(counts, spread, preferred_element_type=f32)[0:1]
    live = (lax.broadcasted_iota(jnp.int32, (1, TAILS), 1) % TAIL).astype(f32) < tail_count
    fill(rows, pl.ds(0, TAILS), pl.ds(NEAR, TAILS), live)
    columns[...] = rows[...].T
    for k in range(16):
        flat[:, 8 * k : 8 * k + 8] = columns[pl.ds(k, N_SLAB, stride=16), :]
    for p in range(N_PENCIL):
        for k in range(8):
            tail_ref[p, :, 16 * k : 16 * k + 16] = flat[8 * k : 8 * k + 8, 16 * p : 16 * p + 16]
    for group in range(9):
        live = lax.broadcasted_iota(jnp.int32, (1, CAP), 1) < counts_smem[0, group]
        fill((left_ref, mid_ref, right_ref)[group % 3], pl.ds(group // 3 * CAP, CAP), pl.ds(group * CAP, CAP), live)


def pack(counts, cells, fractions, adjoint_pos, adjoint_vel):
    field = pltpu.VMEM(fractions.shape, f32)
    side = jax.ShapeDtypeStruct((8, 3 * CAP), f32)
    return pl.pallas_call(
        pack_kernel,
        out_shape=(jax.ShapeDtypeStruct((N_PENCIL, 8, 128), f32), side, side, side),
        in_specs=[SMEM] + [HBM] * 5,
        out_specs=(VMEM,) * 4,
        scratch_shapes=[
            pltpu.VMEM(counts.shape, jnp.int32),
            pltpu.VMEM(cells.shape, jnp.int32),
            field,
            field,
            field,
            pltpu.VMEM((8, TAILS), f32),
            pltpu.VMEM((TAILS, 8), f32),
            pltpu.VMEM((N_SLAB, 128), f32),
            pltpu.SemaphoreType.DMA((5,)),
        ],
        compiler_params=WIDE,
        name="pack",
    )(counts, counts, cells, fractions, adjoint_pos, adjoint_vel)


def repack_kernel(in_ref, out_ref, flat):
    for p in range(N_PENCIL):
        for k in range(8):
            flat[8 * k : 8 * k + 8, 16 * p : 16 * p + 16] = in_ref[p, :, 16 * k : 16 * k + 16]
    out_ref[pl.ds(0, N_SLAB, stride=2), :] = flat[...]
    out_ref[pl.ds(1, N_SLAB, stride=2), :] = jnp.concatenate([flat[N_SLAB - 1 :], flat[: N_SLAB - 1]], axis=0)


def repack(tail):
    return pl.pallas_call(
        repack_kernel,
        out_shape=jax.ShapeDtypeStruct((2 * N_SLAB, 128), f32),
        in_specs=[VMEM],
        out_specs=VMEM,
        scratch_shapes=[pltpu.VMEM((N_SLAB, 128), f32)],
        compiler_params=PARAMS,
        name="repack",
    )(tail)


def paint(values, acc_ref, below=None, spill=False):
    slots = values.shape[1]
    cell = values[0:1].astype(jnp.int32)
    row = lax.shift_right_logical(cell, 13) * STRIDE + (lax.shift_right_logical(cell, 8) & 31)
    if spill:
        row = row - MAIN
    if below is not None:
        row = row - below
    base_z = cell & 255
    next_z = (base_z + 1) & 255
    frac_x, frac_y, frac_z = values[1:2], values[2:3], values[3:4]
    rest_x, rest_y, rest_z = 1.0 - frac_x, 1.0 - frac_y, 1.0 - frac_z
    zero = jnp.zeros((), bf16)

    def short(value):
        return value.astype(f32).astype(bf16)

    count = 48 if spill else MAIN
    row_ids = short(lax.broadcasted_iota(jnp.int32, (count, slots), 0))
    corner = jnp.where(row_ids == short(row + STRIDE), short(frac_x * rest_y), zero)
    corner = jnp.where(row_ids == short(row + STRIDE + 1), short(frac_x * frac_y), corner)
    if not spill:
        corner = jnp.where(row_ids == short(row), short(rest_x * rest_y), corner)
        corner = jnp.where(row_ids == short(row + 1), short(rest_x * frac_y), corner)
    z_ids = short(lax.broadcasted_iota(jnp.int32, (NG, slots), 0))
    at_low, at_high = z_ids == short(base_z), z_ids == short(next_z)
    for i in range(3):
        weight = values[4 + i : 5 + i]
        line = jnp.where(at_low, short(weight * rest_z), zero)
        line = jnp.where(at_high, short(weight * frac_z), line)
        acc_ref[:count, i * NG : (i + 1) * NG] += lax.dot_general(
            corner, line, (((1,), (1,)), ((), ())), preferred_element_type=f32
        )


def near_kernel(below2_ref, below_ref, left_ref, mid_ref, right_ref, above_ref, out_ref):
    out_ref[...] = jnp.zeros_like(out_ref)
    for ref in (left_ref, mid_ref, right_ref):
        paint(ref[:, CAP : 2 * CAP], out_ref)
        paint(ref[:, :CAP], out_ref, spill=True)

    def body(step, carry):
        at = pl.multiple_of(step * CAP, CAP)
        paint(above_ref[:, pl.ds(at, CAP)], out_ref)
        paint(below2_ref[:, pl.ds(at, CAP)], out_ref, spill=True)
        paint(below_ref[:, pl.ds(2 * at, CAP)], out_ref, spill=True)
        paint(below_ref[:, pl.ds(2 * at + CAP, CAP)], out_ref)
        return carry

    lax.fori_loop(0, 3, body, 0)


def paint_near(below2, below, left, mid, right, above):
    return pl.pallas_call(
        near_kernel,
        out_shape=jax.ShapeDtypeStruct((MAIN, 3 * NG), f32),
        in_specs=[VMEM] * 6,
        out_specs=VMEM,
        compiler_params=PARAMS,
        cost_estimate=pl.CostEstimate(flops=4 * NEAR * MAIN * 3 * NG, bytes_accessed=2_000_000, transcendentals=0),
        name="paint_near",
    )(below2, below, left, mid, right, above)


def tail_kernel(tail_ref, near_ref, out_ref, values):
    turned = tail_ref[...].T
    for k in range(16):
        values[:, 128 * k : 128 * k + 128] = turned[8 * k : 8 * k + 8, :]
    out_ref[...] = near_ref[...]
    below = lax.broadcasted_iota(jnp.int32, (1, CAP), 1) % 2 * MAIN

    def body(step, carry):
        for half in range(2):
            at = pl.ds(pl.multiple_of((2 * step + half) * CAP, CAP), CAP)
            paint(values[:, at], out_ref, below)
        return carry

    lax.fori_loop(0, 2, body, 0)


def paint_tail(tail, near):
    return pl.pallas_call(
        tail_kernel,
        out_shape=jax.ShapeDtypeStruct((MAIN, 3 * NG), f32),
        in_specs=[VMEM] * 2,
        out_specs=VMEM,
        scratch_shapes=[pltpu.VMEM((8, 2 * TAILS), f32)],
        compiler_params=PARAMS,
        name="paint_tail",
    )(tail, near)


def z_kernel(main_ref, plain_high, plain_low, scaled_high, scaled_low, out_ref):
    for i in range(3):
        data = main_ref[:, i * NG : (i + 1) * NG]
        high = data.astype(bf16)
        low = (data - high.astype(f32)).astype(bf16)
        table_high, table_low = (scaled_high, scaled_low) if i == 2 else (plain_high, plain_low)
        dot = functools.partial(jnp.dot, preferred_element_type=f32)
        result = dot(high, table_high[...]) + (dot(low, table_high[...]) + dot(high, table_low[...]))
        for part in range(2):
            block = 2 * i + part
            for p in range(N_PENCIL):
                at = part * NG + p * 32
                chunk = jnp.concatenate(
                    [result[x * STRIDE : (x + 1) * STRIDE, at : at + 32] for x in range(CX)], axis=1
                )
                out_ref[p, block * CY : (block + 1) * CY, :] = chunk[:CY]
                out_ref[p, 6 * CY + block : 6 * CY + block + 1, :] = chunk[CY : CY + 1]
    out_ref[:, 6 * CY + 6 :, :] = jnp.zeros((N_PENCIL, 2, 128), f32)


def transform_z(main, plain, scaled):
    return pl.pallas_call(
        z_kernel,
        out_shape=jax.ShapeDtypeStruct((N_PENCIL, CHUNK, 128), f32),
        in_specs=[VMEM] * 5,
        out_specs=VMEM,
        compiler_params=PARAMS,
        name="transform_z",
    )(main, *plain, *scaled)


def mixed_rhs(real, imag):
    return jnp.concatenate(
        [jnp.concatenate([real, imag], axis=1), jnp.concatenate([imag, -real], axis=1)], axis=0
    )


def y_kernel(in_ref, table_high, table_low, out_ref):
    first = lax.broadcasted_iota(jnp.int32, (CY, 128), 0) == 0
    blocks = []
    for block in range(6):
        parts = []
        for src in range(N_PENCIL):
            spilled = in_ref[(src - 1) % N_PENCIL, 6 * CY + block : 6 * CY + block + 1, :]
            parts.append(in_ref[src, block * CY : (block + 1) * CY, :] + jnp.where(first, spilled, 0.0))
        blocks.append(jnp.concatenate(parts, axis=0))
    field = product(table_high[:, 2 * NG :], table_low[:, 2 * NG :], mixed_rhs(blocks[0], blocks[1]))
    sides = jnp.concatenate([mixed_rhs(blocks[2], blocks[3]), mixed_rhs(blocks[4], blocks[5])], axis=0)
    mixed = product(table_high[...], table_low[...], sides)
    for f, result in enumerate((field, mixed)):
        for part in range(2):
            for x in range(CX):
                at = part * 128 + x * 32
                chunk = jnp.concatenate(
                    [result[r * N_SLAB : (r + 1) * N_SLAB, at : at + 32] for r in range(4)], axis=1
                )
                out_ref[pl.ds(x * 4 + f * 2 + part, N_SLAB, stride=16), :] = chunk


def transform_y(by_rows, table):
    return pl.pallas_call(
        y_kernel,
        out_shape=jax.ShapeDtypeStruct((N_SLAB * 16, 128), f32),
        in_specs=[VMEM] * 3,
        out_specs=VMEM,
        compiler_params=PARAMS,
        name="transform_y",
    )(by_rows, *table)


def wavenumber(position):
    return jnp.where(position < NG // 2, position, position - NG).astype(f32)


def x_kernel(place_ref, in_ref, table_high, table_low, out_ref):
    lines = [in_ref[pl.ds(block, NG, stride=4), :] for block in range(4)]
    data = jnp.concatenate([mixed_rhs(lines[0], lines[1]), mixed_rhs(lines[2], lines[3])], axis=0)
    mixed = product(table_high[...], table_low[...], data)
    lane = lax.broadcasted_iota(jnp.int32, (1, 128), 1)
    wave_y = wavenumber(place_ref[0] * 4 + lane // 32)
    wave_z = wavenumber(place_ref[1] * 32 + lane % 32)
    wave_x = wavenumber(lax.broadcasted_iota(jnp.int32, (NG, 1), 0))
    wave_sq = wave_x * wave_x + wave_y * wave_y + wave_z * wave_z
    factor = jnp.where(wave_sq > 0, out_scale / jnp.sqrt(jnp.maximum(wave_sq, 1.0)), 0.0) / NG**1.5
    out_ref[0] = (mixed[:, 128:] * factor).T
    out_ref[1] = (mixed[:, :128] * -factor).T


def transform_x(place, by_cols, table):
    return pl.pallas_call(
        x_kernel,
        out_shape=jax.ShapeDtypeStruct((2, 128, NG), f32),
        in_specs=[SMEM] + [VMEM] * 3,
        out_specs=VMEM,
        compiler_params=PARAMS,
        name="transform_x",
    )(place, by_cols, *table)


def local(cells, fractions, adjoint_pos, adjoint_vel, counts):
    plain, scaled, table_y, table_x = [tuple(jnp.asarray(t) for t in pair) for pair in host_tables()]
    arrays = (counts, cells, fractions, adjoint_pos, adjoint_vel)
    tail, to_left, mid, to_right = pack(*arrays)
    from_right = shifted(to_left, "pencil", -1)
    from_left = shifted(to_right, "pencil", 1)
    columns = (from_left, mid, from_right)
    from_below2 = shifted(jnp.concatenate([column[:, 2 * CAP :] for column in columns], axis=1), "slab", 2)
    from_below = shifted(jnp.concatenate([column[:, CAP:] for column in columns], axis=1), "slab", 1)
    from_above = shifted(jnp.concatenate([column[:, :CAP] for column in columns], axis=1), "slab", -1)
    tail = lax.all_to_all(tail, "pencil", 0, 0, tiled=True)
    tail = lax.all_to_all(repack(tail).reshape(N_SLAB, 2, 128), "slab", 0, 0, tiled=True)
    near = paint_near(from_below2, from_below, *columns, from_above)
    main = paint_tail(tail.reshape(2 * N_SLAB, 128), near)
    by_rows = transform_z(main, plain, scaled)
    by_rows = lax.all_to_all(by_rows, "pencil", 0, 0, tiled=True)
    by_cols = transform_y(by_rows, table_y)
    by_cols = lax.all_to_all(by_cols.reshape(N_SLAB, 16, 128), "slab", 0, 0, tiled=True)
    place = jnp.stack([lax.axis_index("slab"), lax.axis_index("pencil")]).astype(jnp.int32)
    result = transform_x(place, by_cols.reshape(N_SLAB * 16, 128), table_x)
    return result.reshape(2, CX, 32, NG)


def solution(mesh):
    in_specs = (
        P(("slab", "pencil"), None),
        P(None, ("slab", "pencil"), None),
        P(None, ("slab", "pencil"), None),
        P(None, ("slab", "pencil"), None),
        P(("slab", "pencil"), None),
    )
    out_specs = P(None, "slab", "pencil", None)
    return jax.shard_map(local, mesh=mesh, in_specs=in_specs, out_specs=out_specs, check_vma=False)
```

```python
import functools

import jax
import jax.numpy as jnp
import ml_dtypes
import numpy as np
from jax import lax
from jax.experimental import pallas as pl
from jax.experimental.pallas import tpu as pltpu
from jax.sharding import PartitionSpec as P

NG = 256
CAP = 512
TAIL = 2
N_SLAB = 64
N_PENCIL = 8
OWNERS = 512
NEAR = 9 * CAP
TAILS = OWNERS * TAIL
CX = 4
CY = 32
STRIDE = 40
MAIN = CX * STRIDE
CHUNK = 6 * CY + 8

kick_factor = 0.8
drift_factor = 1.25
out_scale = 3.0

f32 = jnp.float32
bf16 = jnp.bfloat16
VMEM = pl.BlockSpec(memory_space=pltpu.VMEM)
SMEM = pl.BlockSpec(memory_space=pltpu.SMEM)
HBM = pl.BlockSpec(memory_space=pltpu.HBM)
ANY = pl.BlockSpec(memory_space=pl.ANY)
WIDE = pltpu.CompilerParams(vmem_limit_bytes=60 * 1024 * 1024)
PARAMS = pltpu.CompilerParams(vmem_limit_bytes=24 * 1024 * 1024)


def split_table(table):
    high = table.astype(ml_dtypes.bfloat16)
    low = (table - high.astype(np.float64)).astype(ml_dtypes.bfloat16)
    return high, low


@functools.cache
def host_tables():
    idx = np.arange(NG)
    angles = (idx[:, None] * idx[None, :] % NG) * (2.0 * np.pi / NG)
    cosine, sine = np.cos(angles), np.sin(angles)
    wave = np.where(idx < NG // 2, idx, idx - NG).astype(np.float64)
    table_z = np.concatenate([cosine, -sine], axis=1)
    table_kz = np.concatenate([cosine * wave[None, :], -sine * wave[None, :]], axis=1)
    table_k = np.concatenate([cosine * wave[:, None], sine * wave[:, None], cosine, sine], axis=1)
    order = np.array([4 * s + r for r in range(4) for s in range(N_SLAB)])
    return (
        split_table(table_z),
        split_table(table_kz),
        split_table(table_k[order]),
        split_table(table_k),
    )


def swapped(block, first):
    count = lax.axis_size("slab")
    pairs = [((i + first) % count, (i + first + 1) % count) for i in range(0, count, 2)]
    return lax.ppermute(block, "slab", pairs + [(b, a) for a, b in pairs])


def shifted(block, axis, distance):
    devices = range(lax.axis_size(axis))
    route = [((i - distance) % len(devices), i) for i in devices]
    return lax.ppermute(block, axis, route)


def product(table_high, table_low, data):
    high = data.astype(bf16)
    low = (data - high.astype(f32)).astype(bf16)
    dot = functools.partial(jnp.dot, preferred_element_type=f32)
    return dot(table_high, high) + (dot(table_high, low) + dot(table_low, high))


def start_copies(pairs, sems):
    copies = [pltpu.make_async_copy(src, dst, sems.at[i]) for i, (src, dst) in enumerate(pairs)]
    for copy in copies:
        copy.start()
    return copies


def particle_rows(out, lanes, live, cells, frac, pos, vel):
    out[0:1, lanes] = cells.astype(f32)
    for i in range(3):
        out[1 + i : 2 + i, lanes] = frac[i]
        weight = kick_factor * (vel[i] + drift_factor * pos[i])
        out[4 + i : 5 + i, lanes] = jnp.where(live, weight, 0.0)
    out[7:8, lanes] = jnp.zeros(cells.shape, f32)


def pack_kernel(counts_hbm, cells_hbm, frac_hbm, pos_hbm, vel_hbm, tail_ref, left_ref, mid_ref, right_ref, counts_ref, cells_ref, frac_ref, pos_ref, vel_ref, counts_smem, rows, columns, flat, sems):
    copies = start_copies(
        [(counts_hbm, counts_ref), (counts_hbm, counts_smem), (cells_hbm, cells_ref), (frac_hbm, frac_ref), (pos_hbm, pos_ref), (vel_hbm, vel_ref)], sems
    )
    width = counts_ref.shape[1]
    slot_of = lax.broadcasted_iota(jnp.int32, (width, TAILS), 1)
    entry = lax.broadcasted_iota(jnp.int32, (width, TAILS), 0)
    spread = jnp.where(slot_of // TAIL + 9 == entry, 1.0, 0.0).astype(bf16)
    for copy in copies:
        copy.wait()

    def fill(out, lanes, src, live):
        particle_rows(out, lanes, live, cells_ref[:, src], frac_ref[:, :, src], pos_ref[:, :, src], vel_ref[:, :, src])

    counts = jnp.broadcast_to(counts_ref[...].astype(f32), (8, width)).astype(bf16)
    tail_count = jnp.dot(counts, spread, preferred_element_type=f32)[0:1]
    live = (lax.broadcasted_iota(jnp.int32, (1, TAILS), 1) % TAIL).astype(f32) < tail_count
    fill(rows, pl.ds(0, TAILS), pl.ds(NEAR, TAILS), live)
    columns[...] = rows[...].T
    for k in range(16):
        flat[:, 8 * k : 8 * k + 8] = columns[pl.ds(k, N_SLAB, stride=16), :]
    for p in range(N_PENCIL):
        for k in range(8):
            tail_ref[p, :, 16 * k : 16 * k + 16] = flat[8 * k : 8 * k + 8, 16 * p : 16 * p + 16]
    for group in range(9):
        live = lax.broadcasted_iota(jnp.int32, (1, CAP), 1) < counts_smem[0, group]
        fill((left_ref, mid_ref, right_ref)[group % 3], pl.ds(group // 3 * CAP, CAP), pl.ds(group * CAP, CAP), live)


def pack(counts, cells, fractions, adjoint_pos, adjoint_vel):
    field = pltpu.VMEM(fractions.shape, f32)
    side = jax.ShapeDtypeStruct((8, 3 * CAP), f32)
    return pl.pallas_call(
        pack_kernel,
        out_shape=(jax.ShapeDtypeStruct((N_PENCIL, 8, 128), f32), side, side, side),
        in_specs=[HBM] * 5,
        out_specs=(VMEM,) * 4,
        scratch_shapes=[
            pltpu.VMEM(counts.shape, jnp.int32),
            pltpu.VMEM(cells.shape, jnp.int32),
            field,
            field,
            field,
            pltpu.SMEM(counts.shape, jnp.int32),
            pltpu.VMEM((8, TAILS), f32),
            pltpu.VMEM((TAILS, 8), f32),
            pltpu.VMEM((N_SLAB, 128), f32),
            pltpu.SemaphoreType.DMA((6,)),
        ],
        compiler_params=WIDE,
        name="pack",
    )(counts, cells, fractions, adjoint_pos, adjoint_vel)


def repack_kernel(in_ref, after_ref, out_ref, flat):
    for p in range(N_PENCIL):
        for k in range(8):
            flat[8 * k : 8 * k + 8, 16 * p : 16 * p + 16] = in_ref[p, :, 16 * k : 16 * k + 16]
    out_ref[pl.ds(0, N_SLAB, stride=2), :] = flat[...]
    out_ref[pl.ds(1, N_SLAB, stride=2), :] = jnp.concatenate([flat[N_SLAB - 1 :], flat[: N_SLAB - 1]], axis=0)


def repack(tail, after):
    return pl.pallas_call(
        repack_kernel,
        out_shape=jax.ShapeDtypeStruct((2 * N_SLAB, 128), f32),
        in_specs=[VMEM, ANY],
        out_specs=VMEM,
        scratch_shapes=[pltpu.VMEM((N_SLAB, 128), f32)],
        compiler_params=PARAMS,
        cost_estimate=pl.CostEstimate(flops=3000000000, bytes_accessed=200_000, transcendentals=0),
        name="repack",
    )(tail, after)


def paint(values, acc_ref, below=None, spill=False):
    slots = values.shape[1]
    cell = values[0:1].astype(jnp.int32)
    row = lax.shift_right_logical(cell, 13) * STRIDE + (lax.shift_right_logical(cell, 8) & 31)
    if spill:
        row = row - MAIN
    if below is not None:
        row = row - below
    base_z = cell & 255
    next_z = (base_z + 1) & 255
    frac_x, frac_y, frac_z = values[1:2], values[2:3], values[3:4]
    rest_x, rest_y, rest_z = 1.0 - frac_x, 1.0 - frac_y, 1.0 - frac_z
    zero = jnp.zeros((), bf16)

    def short(value):
        return value.astype(f32).astype(bf16)

    count = 48 if spill else MAIN
    row_ids = short(lax.broadcasted_iota(jnp.int32, (count, slots), 0))
    corner = jnp.where(row_ids == short(row + STRIDE), short(frac_x * rest_y), zero)
    corner = jnp.where(row_ids == short(row + STRIDE + 1), short(frac_x * frac_y), corner)
    if not spill:
        corner = jnp.where(row_ids == short(row), short(rest_x * rest_y), corner)
        corner = jnp.where(row_ids == short(row + 1), short(rest_x * frac_y), corner)
    z_ids = short(lax.broadcasted_iota(jnp.int32, (NG, slots), 0))
    at_low, at_high = z_ids == short(base_z), z_ids == short(next_z)
    for i in range(3):
        weight = values[4 + i : 5 + i]
        line = jnp.where(at_low, short(weight * rest_z), zero)
        line = jnp.where(at_high, short(weight * frac_z), line)
        acc_ref[:count, i * NG : (i + 1) * NG] += lax.dot_general(
            corner, line, (((1,), (1,)), ((), ())), preferred_element_type=f32
        )


def near_kernel(held_ref, inner_ref, outer_ref, below2_ref, out_ref):
    out_ref[...] = jnp.zeros_like(out_ref)
    even = lax.axis_index("slab") % 2 == 0

    def body(step, carry):
        def group(ref, index):
            return ref[:, pl.ds(pl.multiple_of((3 * step + index) * CAP, CAP), CAP)]

        def pick(first, then, index):
            return jnp.where(even, group(first, index), group(then, index))

        paint(group(held_ref, 1), out_ref)
        paint(group(held_ref, 0), out_ref, spill=True)
        paint(pick(inner_ref, outer_ref, 0), out_ref)
        paint(pick(outer_ref, inner_ref, 2), out_ref)
        paint(pick(outer_ref, inner_ref, 1), out_ref, spill=True)
        paint(group(below2_ref, 2), out_ref, spill=True)
        return carry

    lax.fori_loop(0, 3, body, 0)


def paint_near(held, inner, outer, below2):
    return pl.pallas_call(
        near_kernel,
        out_shape=jax.ShapeDtypeStruct((MAIN, 3 * NG), f32),
        in_specs=[VMEM] * 4,
        out_specs=VMEM,
        compiler_params=PARAMS,
        cost_estimate=pl.CostEstimate(flops=4 * NEAR * MAIN * 3 * NG, bytes_accessed=2_000_000, transcendentals=0),
        name="paint_near",
    )(held, inner, outer, below2)


def tail_kernel(tail_ref, near_ref, plain_high, plain_low, scaled_high, scaled_low, out_ref, values, painted):
    turned = tail_ref[...].T
    for k in range(16):
        values[:, 128 * k : 128 * k + 128] = turned[8 * k : 8 * k + 8, :]
    painted[...] = near_ref[...]
    below = lax.broadcasted_iota(jnp.int32, (1, CAP), 1) % 2 * MAIN

    def body(step, carry):
        for half in range(2):
            at = pl.ds(pl.multiple_of((2 * step + half) * CAP, CAP), CAP)
            paint(values[:, at], painted, below)
        return carry

    lax.fori_loop(0, 2, body, 0)
    for i in range(3):
        data = painted[:, i * NG : (i + 1) * NG]
        high = data.astype(bf16)
        low = (data - high.astype(f32)).astype(bf16)
        table_high, table_low = (scaled_high, scaled_low) if i == 2 else (plain_high, plain_low)
        dot = functools.partial(jnp.dot, preferred_element_type=f32)
        result = dot(high, table_high[...]) + (dot(low, table_high[...]) + dot(high, table_low[...]))
        for part in range(2):
            block = 2 * i + part
            for p in range(N_PENCIL):
                at = part * NG + p * 32
                chunk = jnp.concatenate(
                    [result[x * STRIDE : (x + 1) * STRIDE, at : at + 32] for x in range(CX)], axis=1
                )
                out_ref[p, block * CY : (block + 1) * CY, :] = chunk[:CY]
                out_ref[p, 6 * CY + block : 6 * CY + block + 1, :] = chunk[CY : CY + 1]
    out_ref[:, 6 * CY + 6 :, :] = jnp.zeros((N_PENCIL, 2, 128), f32)


def paint_tail_transform_z(tail, near, plain, scaled):
    return pl.pallas_call(
        tail_kernel,
        out_shape=jax.ShapeDtypeStruct((N_PENCIL, CHUNK, 128), f32),
        in_specs=[VMEM] * 6,
        out_specs=VMEM,
        scratch_shapes=[pltpu.VMEM((8, 2 * TAILS), f32), pltpu.VMEM((MAIN, 3 * NG), f32)],
        compiler_params=PARAMS,
        name="paint_tail_transform_z",
    )(tail, near, *plain, *scaled)


def mixed_rhs(real, imag):
    return jnp.concatenate(
        [jnp.concatenate([real, imag], axis=1), jnp.concatenate([imag, -real], axis=1)], axis=0
    )


def y_kernel(in_ref, table_high, table_low, out_ref):
    first = lax.broadcasted_iota(jnp.int32, (CY, 128), 0) == 0
    blocks = []
    for block in range(6):
        parts = []
        for src in range(N_PENCIL):
            spilled = in_ref[(src - 1) % N_PENCIL, 6 * CY + block : 6 * CY + block + 1, :]
            parts.append(in_ref[src, block * CY : (block + 1) * CY, :] + jnp.where(first, spilled, 0.0))
        blocks.append(jnp.concatenate(parts, axis=0))
    field = product(table_high[:, 2 * NG :], table_low[:, 2 * NG :], mixed_rhs(blocks[0], blocks[1]))
    sides = jnp.concatenate([mixed_rhs(blocks[2], blocks[3]), mixed_rhs(blocks[4], blocks[5])], axis=0)
    mixed = product(table_high[...], table_low[...], sides)
    for f, result in enumerate((field, mixed)):
        for part in range(2):
            for x in range(CX):
                at = part * 128 + x * 32
                chunk = jnp.concatenate(
                    [result[r * N_SLAB : (r + 1) * N_SLAB, at : at + 32] for r in range(4)], axis=1
                )
                out_ref[pl.ds(x * 4 + f * 2 + part, N_SLAB, stride=16), :] = chunk


def transform_y(by_rows, table):
    return pl.pallas_call(
        y_kernel,
        out_shape=jax.ShapeDtypeStruct((N_SLAB * 16, 128), f32),
        in_specs=[VMEM] * 3,
        out_specs=VMEM,
        compiler_params=PARAMS,
        name="transform_y",
    )(by_rows, *table)


def wavenumber(position):
    return jnp.where(position < NG // 2, position, position - NG).astype(f32)


def x_kernel(in_ref, table_high, table_low, out_ref):
    lines = [in_ref[pl.ds(block, NG, stride=4), :] for block in range(4)]
    data = jnp.concatenate([mixed_rhs(lines[0], lines[1]), mixed_rhs(lines[2], lines[3])], axis=0)
    mixed = product(table_high[...], table_low[...], data)
    lane = lax.broadcasted_iota(jnp.int32, (1, 128), 1)
    wave_y = wavenumber(lax.axis_index("slab") * 4 + lane // 32)
    wave_z = wavenumber(lax.axis_index("pencil") * 32 + lane % 32)
    wave_x = wavenumber(lax.broadcasted_iota(jnp.int32, (NG, 1), 0))
    wave_sq = wave_x * wave_x + wave_y * wave_y + wave_z * wave_z
    factor = jnp.where(wave_sq > 0, out_scale / jnp.sqrt(jnp.maximum(wave_sq, 1.0)), 0.0) / NG**1.5
    out_ref[0] = (mixed[:, 128:] * factor).T
    out_ref[1] = (mixed[:, :128] * -factor).T


def transform_x(by_cols, table):
    return pl.pallas_call(
        x_kernel,
        out_shape=jax.ShapeDtypeStruct((2, 128, NG), f32),
        in_specs=[VMEM] * 3,
        out_specs=VMEM,
        compiler_params=PARAMS,
        name="transform_x",
    )(by_cols, *table)


def local(cells, fractions, adjoint_pos, adjoint_vel, counts):
    plain, scaled, table_y, table_x = [tuple(jnp.asarray(t) for t in pair) for pair in host_tables()]
    arrays = (counts, cells, fractions, adjoint_pos, adjoint_vel)
    tail, to_left, mid, to_right = pack(*arrays)
    from_right = shifted(to_left, "pencil", -1)
    from_left = shifted(to_right, "pencil", 1)
    columns = (from_left, mid, from_right)
    held = jnp.concatenate(columns, axis=1)
    inner = swapped(held, 0)
    outer = swapped(held, 1)
    from_below2 = shifted(held, "slab", 2)
    tail = lax.all_to_all(tail, "pencil", 0, 0, tiled=True)
    tail = lax.all_to_all(repack(tail, inner).reshape(N_SLAB, 2, 128), "slab", 0, 0, tiled=True)
    near = paint_near(held, inner, outer, from_below2)
    by_rows = paint_tail_transform_z(tail.reshape(2 * N_SLAB, 128), near, plain, scaled)
    by_rows = lax.all_to_all(by_rows, "pencil", 0, 0, tiled=True)
    by_cols = transform_y(by_rows, table_y)
    by_cols = lax.all_to_all(by_cols.reshape(N_SLAB, 16, 128), "slab", 0, 0, tiled=True)
    result = transform_x(by_cols.reshape(N_SLAB * 16, 128), table_x)
    return result.reshape(2, CX, 32, NG)


def solution(mesh):
    in_specs = (
        P(("slab", "pencil"), None),
        P(None, ("slab", "pencil"), None),
        P(None, ("slab", "pencil"), None),
        P(None, ("slab", "pencil"), None),
        P(("slab", "pencil"), None),
    )
    out_specs = P(None, "slab", "pencil", None)
    return jax.shard_map(local, mesh=mesh, in_specs=in_specs, out_specs=out_specs, check_vma=False)
```

```python
import functools

import jax
import jax.numpy as jnp
import ml_dtypes
import numpy as np
from jax import lax
from jax.experimental import pallas as pl
from jax.experimental.pallas import tpu as pltpu
from jax.sharding import PartitionSpec as P

NG = 256
CAP = 512
TAIL = 2
N_SLAB = 64
N_PENCIL = 8
OWNERS = 512
NEAR = 9 * CAP
TAILS = OWNERS * TAIL
CX = 4
CY = 32
STRIDE = 40
MAIN = CX * STRIDE
CHUNK = 6 * CY + 8

kick_factor = 0.8
drift_factor = 1.25
out_scale = 3.0

f32 = jnp.float32
bf16 = jnp.bfloat16
VMEM = pl.BlockSpec(memory_space=pltpu.VMEM)
SMEM = pl.BlockSpec(memory_space=pltpu.SMEM)
HBM = pl.BlockSpec(memory_space=pltpu.HBM)
ANY = pl.BlockSpec(memory_space=pl.ANY)
WIDE = pltpu.CompilerParams(vmem_limit_bytes=60 * 1024 * 1024)
PARAMS = pltpu.CompilerParams(vmem_limit_bytes=24 * 1024 * 1024)


def split_table(table):
    high = table.astype(ml_dtypes.bfloat16)
    low = (table - high.astype(np.float64)).astype(ml_dtypes.bfloat16)
    return high, low


@functools.cache
def host_tables():
    idx = np.arange(NG)
    angles = (idx[:, None] * idx[None, :] % NG) * (2.0 * np.pi / NG)
    cosine, sine = np.cos(angles), np.sin(angles)
    wave = np.where(idx < NG // 2, idx, idx - NG).astype(np.float64)
    table_z = np.concatenate([cosine, -sine], axis=1)
    table_kz = np.concatenate([cosine * wave[None, :], -sine * wave[None, :]], axis=1)
    table_k = np.concatenate([cosine * wave[:, None], sine * wave[:, None], cosine, sine], axis=1)
    order = np.array([4 * s + r for r in range(4) for s in range(N_SLAB)])
    return (
        split_table(table_z),
        split_table(table_kz),
        split_table(table_k[order]),
        split_table(table_k),
    )


def swapped(block, first):
    count = lax.axis_size("slab")
    pairs = [((i + first) % count, (i + first + 1) % count) for i in range(0, count, 2)]
    return lax.ppermute(block, "slab", pairs + [(b, a) for a, b in pairs])


def shifted(block, axis, distance):
    devices = range(lax.axis_size(axis))
    route = [((i - distance) % len(devices), i) for i in devices]
    return lax.ppermute(block, axis, route)


def product(table_high, table_low, data):
    high = data.astype(bf16)
    low = (data - high.astype(f32)).astype(bf16)
    dot = functools.partial(jnp.dot, preferred_element_type=f32)
    return dot(table_high, high) + (dot(table_high, low) + dot(table_low, high))


def start_copies(pairs, sems):
    copies = [pltpu.make_async_copy(src, dst, sems.at[i]) for i, (src, dst) in enumerate(pairs)]
    for copy in copies:
        copy.start()
    return copies


def particle_rows(out, lanes, live, cells, frac, pos, vel):
    out[0:1, lanes] = cells.astype(f32)
    for i in range(3):
        out[1 + i : 2 + i, lanes] = frac[i]
        weight = kick_factor * (vel[i] + drift_factor * pos[i])
        out[4 + i : 5 + i, lanes] = jnp.where(live, weight, 0.0)
    out[7:8, lanes] = jnp.zeros(cells.shape, f32)


def pack_kernel(counts_hbm, cells_hbm, frac_hbm, pos_hbm, vel_hbm, tail_ref, left_ref, mid_ref, right_ref, counts_ref, cells_ref, frac_ref, pos_ref, vel_ref, counts_smem, rows, columns, flat, sems):
    copies = start_copies(
        [(counts_hbm, counts_ref), (counts_hbm, counts_smem), (cells_hbm, cells_ref), (frac_hbm, frac_ref), (pos_hbm, pos_ref), (vel_hbm, vel_ref)], sems
    )
    width = counts_ref.shape[1]
    slot_of = lax.broadcasted_iota(jnp.int32, (width, TAILS), 1)
    entry = lax.broadcasted_iota(jnp.int32, (width, TAILS), 0)
    spread = jnp.where(slot_of // TAIL + 9 == entry, 1.0, 0.0).astype(bf16)
    for copy in copies:
        copy.wait()

    def fill(out, lanes, src, live):
        particle_rows(out, lanes, live, cells_ref[:, src], frac_ref[:, :, src], pos_ref[:, :, src], vel_ref[:, :, src])

    counts = jnp.broadcast_to(counts_ref[...].astype(f32), (8, width)).astype(bf16)
    tail_count = jnp.dot(counts, spread, preferred_element_type=f32)[0:1]
    live = (lax.broadcasted_iota(jnp.int32, (1, TAILS), 1) % TAIL).astype(f32) < tail_count
    fill(rows, pl.ds(0, TAILS), pl.ds(NEAR, TAILS), live)
    columns[...] = rows[...].T
    for k in range(16):
        flat[:, 8 * k : 8 * k + 8] = columns[pl.ds(k, N_SLAB, stride=16), :]
    for p in range(N_PENCIL):
        for k in range(8):
            tail_ref[p, :, 16 * k : 16 * k + 16] = flat[8 * k : 8 * k + 8, 16 * p : 16 * p + 16]
    for group in range(9):
        live = lax.broadcasted_iota(jnp.int32, (1, CAP), 1) < counts_smem[0, group]
        fill((left_ref, mid_ref, right_ref)[group % 3], pl.ds(group // 3 * CAP, CAP), pl.ds(group * CAP, CAP), live)


def pack(counts, cells, fractions, adjoint_pos, adjoint_vel):
    field = pltpu.VMEM(fractions.shape, f32)
    side = jax.ShapeDtypeStruct((8, 3 * CAP), f32)
    return pl.pallas_call(
        pack_kernel,
        out_shape=(jax.ShapeDtypeStruct((N_PENCIL, 8, 128), f32), side, side, side),
        in_specs=[HBM] * 5,
        out_specs=(VMEM,) * 4,
        scratch_shapes=[
            pltpu.VMEM(counts.shape, jnp.int32),
            pltpu.VMEM(cells.shape, jnp.int32),
            field,
            field,
            field,
            pltpu.SMEM(counts.shape, jnp.int32),
            pltpu.VMEM((8, TAILS), f32),
            pltpu.VMEM((TAILS, 8), f32),
            pltpu.VMEM((N_SLAB, 128), f32),
            pltpu.SemaphoreType.DMA((6,)),
        ],
        compiler_params=WIDE,
        name="pack",
    )(counts, cells, fractions, adjoint_pos, adjoint_vel)


def repack_kernel(in_ref, after_ref, out_ref, flat):
    for p in range(N_PENCIL):
        for k in range(8):
            flat[8 * k : 8 * k + 8, 16 * p : 16 * p + 16] = in_ref[p, :, 16 * k : 16 * k + 16]
    out_ref[pl.ds(0, N_SLAB, stride=2), :] = flat[...]
    out_ref[pl.ds(1, N_SLAB, stride=2), :] = jnp.concatenate([flat[N_SLAB - 1 :], flat[: N_SLAB - 1]], axis=0)


def repack(tail, after):
    return pl.pallas_call(
        repack_kernel,
        out_shape=jax.ShapeDtypeStruct((2 * N_SLAB, 128), f32),
        in_specs=[VMEM, ANY],
        out_specs=VMEM,
        scratch_shapes=[pltpu.VMEM((N_SLAB, 128), f32)],
        compiler_params=PARAMS,
        cost_estimate=pl.CostEstimate(flops=3000000000, bytes_accessed=200_000, transcendentals=0),
        name="repack",
    )(tail, after)


def paint(values, acc_ref, below=None, spill=False):
    slots = values.shape[1]
    cell = values[0:1].astype(jnp.int32)
    row = lax.shift_right_logical(cell, 13) * STRIDE + (lax.shift_right_logical(cell, 8) & 31)
    if spill:
        row = row - MAIN
    if below is not None:
        row = row - below
    base_z = cell & 255
    next_z = (base_z + 1) & 255
    frac_x, frac_y, frac_z = values[1:2], values[2:3], values[3:4]
    rest_x, rest_y, rest_z = 1.0 - frac_x, 1.0 - frac_y, 1.0 - frac_z
    zero = jnp.zeros((), bf16)

    def short(value):
        return value.astype(f32).astype(bf16)

    count = 48 if spill else MAIN
    row_ids = short(lax.broadcasted_iota(jnp.int32, (count, slots), 0))
    corner = jnp.where(row_ids == short(row + STRIDE), short(frac_x * rest_y), zero)
    corner = jnp.where(row_ids == short(row + STRIDE + 1), short(frac_x * frac_y), corner)
    if not spill:
        corner = jnp.where(row_ids == short(row), short(rest_x * rest_y), corner)
        corner = jnp.where(row_ids == short(row + 1), short(rest_x * frac_y), corner)
    z_ids = short(lax.broadcasted_iota(jnp.int32, (NG, slots), 0))
    at_low, at_high = z_ids == short(base_z), z_ids == short(next_z)
    for i in range(3):
        weight = values[4 + i : 5 + i]
        line = jnp.where(at_low, short(weight * rest_z), zero)
        line = jnp.where(at_high, short(weight * frac_z), line)
        acc_ref[:count, i * NG : (i + 1) * NG] += lax.dot_general(
            corner, line, (((1,), (1,)), ((), ())), preferred_element_type=f32
        )


def near_kernel(held_ref, inner_ref, outer_ref, below2_ref, out_ref):
    out_ref[...] = jnp.zeros_like(out_ref)
    even = lax.axis_index("slab") % 2 == 0

    def body(step, carry):
        def group(ref, index):
            return ref[:, pl.ds(pl.multiple_of((3 * step + index) * CAP, CAP), CAP)]

        def pick(first, then, index):
            return jnp.where(even, group(first, index), group(then, index))

        paint(group(held_ref, 1), out_ref)
        paint(group(held_ref, 0), out_ref, spill=True)
        paint(pick(inner_ref, outer_ref, 0), out_ref)
        paint(pick(outer_ref, inner_ref, 2), out_ref)
        paint(pick(outer_ref, inner_ref, 1), out_ref, spill=True)
        paint(below2_ref[:, pl.ds(pl.multiple_of(step * CAP, CAP), CAP)], out_ref, spill=True)
        return carry

    lax.fori_loop(0, 3, body, 0)


def paint_near(held, inner, outer, below2):
    return pl.pallas_call(
        near_kernel,
        out_shape=jax.ShapeDtypeStruct((MAIN, 3 * NG), f32),
        in_specs=[VMEM] * 4,
        out_specs=VMEM,
        compiler_params=PARAMS,
        cost_estimate=pl.CostEstimate(flops=9059696640, bytes_accessed=2_000_000, transcendentals=0),
        name="paint_near",
    )(held, inner, outer, below2)


def tail_kernel(tail_ref, near_ref, plain_high, plain_low, scaled_high, scaled_low, out_ref, values, painted):
    turned = tail_ref[...].T
    for k in range(16):
        values[:, 128 * k : 128 * k + 128] = turned[8 * k : 8 * k + 8, :]
    painted[...] = near_ref[...]
    below = lax.broadcasted_iota(jnp.int32, (1, CAP), 1) % 2 * MAIN

    def body(step, carry):
        for half in range(2):
            at = pl.ds(pl.multiple_of((2 * step + half) * CAP, CAP), CAP)
            paint(values[:, at], painted, below)
        return carry

    lax.fori_loop(0, 2, body, 0)
    for i in range(3):
        data = painted[:, i * NG : (i + 1) * NG]
        high = data.astype(bf16)
        low = (data - high.astype(f32)).astype(bf16)
        table_high, table_low = (scaled_high, scaled_low) if i == 2 else (plain_high, plain_low)
        dot = functools.partial(jnp.dot, preferred_element_type=f32)
        result = dot(high, table_high[...]) + (dot(low, table_high[...]) + dot(high, table_low[...]))
        for part in range(2):
            block = 2 * i + part
            for p in range(N_PENCIL):
                at = part * NG + p * 32
                chunk = jnp.concatenate(
                    [result[x * STRIDE : (x + 1) * STRIDE, at : at + 32] for x in range(CX)], axis=1
                )
                out_ref[p, block * CY : (block + 1) * CY, :] = chunk[:CY]
                out_ref[p, 6 * CY + block : 6 * CY + block + 1, :] = chunk[CY : CY + 1]
    out_ref[:, 6 * CY + 6 :, :] = jnp.zeros((N_PENCIL, 2, 128), f32)


def paint_tail_transform_z(tail, near, plain, scaled):
    return pl.pallas_call(
        tail_kernel,
        out_shape=jax.ShapeDtypeStruct((N_PENCIL, CHUNK, 128), f32),
        in_specs=[VMEM] * 6,
        out_specs=VMEM,
        scratch_shapes=[pltpu.VMEM((8, 2 * TAILS), f32), pltpu.VMEM((MAIN, 3 * NG), f32)],
        compiler_params=PARAMS,
        name="paint_tail_transform_z",
    )(tail, near, *plain, *scaled)


def mixed_rhs(real, imag):
    return jnp.concatenate(
        [jnp.concatenate([real, imag], axis=1), jnp.concatenate([imag, -real], axis=1)], axis=0
    )


def y_kernel(in_ref, table_high, table_low, out_ref):
    first = lax.broadcasted_iota(jnp.int32, (CY, 128), 0) == 0
    blocks = []
    for block in range(6):
        parts = []
        for src in range(N_PENCIL):
            spilled = in_ref[(src - 1) % N_PENCIL, 6 * CY + block : 6 * CY + block + 1, :]
            parts.append(in_ref[src, block * CY : (block + 1) * CY, :] + jnp.where(first, spilled, 0.0))
        blocks.append(jnp.concatenate(parts, axis=0))
    field = product(table_high[:, 2 * NG :], table_low[:, 2 * NG :], mixed_rhs(blocks[0], blocks[1]))
    sides = jnp.concatenate([mixed_rhs(blocks[2], blocks[3]), mixed_rhs(blocks[4], blocks[5])], axis=0)
    mixed = product(table_high[...], table_low[...], sides)
    for f, result in enumerate((field, mixed)):
        for part in range(2):
            for x in range(CX):
                at = part * 128 + x * 32
                chunk = jnp.concatenate(
                    [result[r * N_SLAB : (r + 1) * N_SLAB, at : at + 32] for r in range(4)], axis=1
                )
                out_ref[pl.ds(x * 4 + f * 2 + part, N_SLAB, stride=16), :] = chunk


def transform_y(by_rows, table):
    return pl.pallas_call(
        y_kernel,
        out_shape=jax.ShapeDtypeStruct((N_SLAB * 16, 128), f32),
        in_specs=[VMEM] * 3,
        out_specs=VMEM,
        compiler_params=PARAMS,
        name="transform_y",
    )(by_rows, *table)


def wavenumber(position):
    return jnp.where(position < NG // 2, position, position - NG).astype(f32)


def x_kernel(in_ref, table_high, table_low, out_ref):
    lines = [in_ref[pl.ds(block, NG, stride=4), :] for block in range(4)]
    data = jnp.concatenate([mixed_rhs(lines[0], lines[1]), mixed_rhs(lines[2], lines[3])], axis=0)
    mixed = product(table_high[...], table_low[...], data)
    lane = lax.broadcasted_iota(jnp.int32, (1, 128), 1)
    wave_y = wavenumber(lax.axis_index("slab") * 4 + lane // 32)
    wave_z = wavenumber(lax.axis_index("pencil") * 32 + lane % 32)
    wave_x = wavenumber(lax.broadcasted_iota(jnp.int32, (NG, 1), 0))
    wave_sq = wave_x * wave_x + wave_y * wave_y + wave_z * wave_z
    factor = jnp.where(wave_sq > 0, out_scale / jnp.sqrt(jnp.maximum(wave_sq, 1.0)), 0.0) / NG**1.5
    out_ref[0] = (mixed[:, 128:] * factor).T
    out_ref[1] = (mixed[:, :128] * -factor).T


def transform_x(by_cols, table):
    return pl.pallas_call(
        x_kernel,
        out_shape=jax.ShapeDtypeStruct((2, 128, NG), f32),
        in_specs=[VMEM] * 3,
        out_specs=VMEM,
        compiler_params=PARAMS,
        name="transform_x",
    )(by_cols, *table)


def local(cells, fractions, adjoint_pos, adjoint_vel, counts):
    plain, scaled, table_y, table_x = [tuple(jnp.asarray(t) for t in pair) for pair in host_tables()]
    arrays = (counts, cells, fractions, adjoint_pos, adjoint_vel)
    tail, to_left, mid, to_right = pack(*arrays)
    from_right = shifted(to_left, "pencil", -1)
    from_left = shifted(to_right, "pencil", 1)
    columns = (from_left, mid, from_right)
    held = jnp.concatenate(columns, axis=1)
    inner = swapped(held, 0)
    outer = swapped(held, 1)
    from_below2 = shifted(jnp.concatenate([held[:, (3 * c + 2) * CAP : (3 * c + 3) * CAP] for c in range(3)], axis=1), "slab", 2)
    tail = lax.all_to_all(tail, "pencil", 0, 0, tiled=True)
    tail = lax.all_to_all(repack(tail, from_below2).reshape(N_SLAB, 2, 128), "slab", 0, 0, tiled=True)
    near = paint_near(held, inner, outer, from_below2)
    by_rows = paint_tail_transform_z(tail.reshape(2 * N_SLAB, 128), near, plain, scaled)
    by_rows = lax.all_to_all(by_rows, "pencil", 0, 0, tiled=True)
    by_cols = transform_y(by_rows, table_y)
    by_cols = lax.all_to_all(by_cols.reshape(N_SLAB, 16, 128), "slab", 0, 0, tiled=True)
    result = transform_x(by_cols.reshape(N_SLAB * 16, 128), table_x)
    return result.reshape(2, CX, 32, NG)


def solution(mesh):
    in_specs = (
        P(("slab", "pencil"), None),
        P(None, ("slab", "pencil"), None),
        P(None, ("slab", "pencil"), None),
        P(None, ("slab", "pencil"), None),
        P(("slab", "pencil"), None),
    )
    out_specs = P(None, "slab", "pencil", None)
    return jax.shard_map(local, mesh=mesh, in_specs=in_specs, out_specs=out_specs, check_vma=False)
```

```python
import functools

import jax
import jax.numpy as jnp
import ml_dtypes
import numpy as np
from jax import lax
from jax.experimental import pallas as pl
from jax.experimental.pallas import tpu as pltpu
from jax.sharding import PartitionSpec as P

NG = 256
CAP = 512
TAIL = 2
N_SLAB = 64
N_PENCIL = 8
OWNERS = 512
NEAR = 9 * CAP
TAILS = OWNERS * TAIL
CX = 4
CY = 32
STRIDE = 40
MAIN = CX * STRIDE
CHUNK = 6 * CY + 8

kick_factor = 0.8
drift_factor = 1.25
out_scale = 3.0

f32 = jnp.float32
bf16 = jnp.bfloat16
VMEM = pl.BlockSpec(memory_space=pltpu.VMEM)
SMEM = pl.BlockSpec(memory_space=pltpu.SMEM)
HBM = pl.BlockSpec(memory_space=pltpu.HBM)
ANY = pl.BlockSpec(memory_space=pl.ANY)
WIDE = pltpu.CompilerParams(vmem_limit_bytes=60 * 1024 * 1024)
PARAMS = pltpu.CompilerParams(vmem_limit_bytes=24 * 1024 * 1024)


def split_table(table):
    high = table.astype(ml_dtypes.bfloat16)
    low = (table - high.astype(np.float64)).astype(ml_dtypes.bfloat16)
    return high, low


@functools.cache
def host_tables():
    idx = np.arange(NG)
    angles = (idx[:, None] * idx[None, :] % NG) * (2.0 * np.pi / NG)
    cosine, sine = np.cos(angles), np.sin(angles)
    wave = np.where(idx < NG // 2, idx, idx - NG).astype(np.float64)
    table_z = np.concatenate([cosine, -sine], axis=1)
    table_kz = np.concatenate([cosine * wave[None, :], -sine * wave[None, :]], axis=1)
    table_k = np.concatenate([cosine * wave[:, None], sine * wave[:, None], cosine, sine], axis=1)
    order = np.array([4 * s + r for r in range(4) for s in range(N_SLAB)])
    return (
        split_table(table_z),
        split_table(table_kz),
        split_table(table_k[order]),
        split_table(table_k),
    )


def swapped(block, first):
    count = lax.axis_size("slab")
    pairs = [((i + first) % count, (i + first + 1) % count) for i in range(0, count, 2)]
    return lax.ppermute(block, "slab", pairs + [(b, a) for a, b in pairs])


def shifted(block, axis, distance):
    devices = range(lax.axis_size(axis))
    route = [((i - distance) % len(devices), i) for i in devices]
    return lax.ppermute(block, axis, route)


def product(table_high, table_low, data):
    high = data.astype(bf16)
    low = (data - high.astype(f32)).astype(bf16)
    dot = functools.partial(jnp.dot, preferred_element_type=f32)
    return dot(table_high, high) + (dot(table_high, low) + dot(table_low, high))


def start_copies(pairs, sems):
    copies = [pltpu.make_async_copy(src, dst, sems.at[i]) for i, (src, dst) in enumerate(pairs)]
    for copy in copies:
        copy.start()
    return copies


def particle_rows(out, lanes, live, cells, frac, pos, vel):
    out[0:1, lanes] = cells.astype(f32)
    for i in range(3):
        out[1 + i : 2 + i, lanes] = frac[i]
        weight = kick_factor * (vel[i] + drift_factor * pos[i])
        out[4 + i : 5 + i, lanes] = jnp.where(live, weight, 0.0)
    out[7:8, lanes] = jnp.zeros(cells.shape, f32)


def pack_kernel(counts_hbm, cells_hbm, frac_hbm, pos_hbm, vel_hbm, tail_ref, left_ref, mid_ref, right_ref, counts_ref, cells_ref, frac_ref, pos_ref, vel_ref, counts_smem, rows, columns, flat, sems):
    copies = start_copies(
        [(counts_hbm, counts_ref), (counts_hbm, counts_smem), (cells_hbm, cells_ref), (frac_hbm, frac_ref), (pos_hbm, pos_ref), (vel_hbm, vel_ref)], sems
    )
    width = counts_ref.shape[1]
    slot_of = lax.broadcasted_iota(jnp.int32, (width, TAILS), 1)
    entry = lax.broadcasted_iota(jnp.int32, (width, TAILS), 0)
    spread = jnp.where(slot_of // TAIL + 9 == entry, 1.0, 0.0).astype(bf16)
    for copy in copies:
        copy.wait()

    def fill(out, lanes, src, live):
        particle_rows(out, lanes, live, cells_ref[:, src], frac_ref[:, :, src], pos_ref[:, :, src], vel_ref[:, :, src])

    counts = jnp.broadcast_to(counts_ref[...].astype(f32), (8, width)).astype(bf16)
    tail_count = jnp.dot(counts, spread, preferred_element_type=f32)[0:1]
    live = (lax.broadcasted_iota(jnp.int32, (1, TAILS), 1) % TAIL).astype(f32) < tail_count
    fill(rows, pl.ds(0, TAILS), pl.ds(NEAR, TAILS), live)
    columns[...] = rows[...].T
    for k in range(16):
        flat[:, 8 * k : 8 * k + 8] = columns[pl.ds(k, N_SLAB, stride=16), :]
    tail_ref[pl.ds(0, N_SLAB, stride=2), :] = flat[...]
    tail_ref[pl.ds(1, N_SLAB, stride=2), :] = jnp.concatenate([flat[N_SLAB - 1 :], flat[: N_SLAB - 1]], axis=0)
    for group in range(9):
        live = lax.broadcasted_iota(jnp.int32, (1, CAP), 1) < counts_smem[0, group]
        fill((left_ref, mid_ref, right_ref)[group % 3], pl.ds(group // 3 * CAP, CAP), pl.ds(group * CAP, CAP), live)


def pack(counts, cells, fractions, adjoint_pos, adjoint_vel):
    field = pltpu.VMEM(fractions.shape, f32)
    side = jax.ShapeDtypeStruct((8, 3 * CAP), f32)
    return pl.pallas_call(
        pack_kernel,
        out_shape=(jax.ShapeDtypeStruct((2 * N_SLAB, 128), f32), side, side, side),
        in_specs=[HBM] * 5,
        out_specs=(VMEM,) * 4,
        scratch_shapes=[
            pltpu.VMEM(counts.shape, jnp.int32),
            pltpu.VMEM(cells.shape, jnp.int32),
            field,
            field,
            field,
            pltpu.SMEM(counts.shape, jnp.int32),
            pltpu.VMEM((8, TAILS), f32),
            pltpu.VMEM((TAILS, 8), f32),
            pltpu.VMEM((N_SLAB, 128), f32),
            pltpu.SemaphoreType.DMA((6,)),
        ],
        compiler_params=WIDE,
        name="pack",
    )(counts, cells, fractions, adjoint_pos, adjoint_vel)


def repack_kernel(in_ref, after_ref, out_ref):
    for which in range(2):
        rows = in_ref[pl.ds(which, N_SLAB, stride=2), :]
        for p in range(N_PENCIL):
            for k in range(8):
                out_ref[p, 8 * which : 8 * which + 8, 16 * k : 16 * k + 16] = rows[8 * k : 8 * k + 8, 16 * p : 16 * p + 16]


def repack(tail, after):
    return pl.pallas_call(
        repack_kernel,
        out_shape=jax.ShapeDtypeStruct((N_PENCIL, 16, 128), f32),
        in_specs=[VMEM, ANY],
        out_specs=VMEM,
        compiler_params=PARAMS,
        cost_estimate=pl.CostEstimate(flops=3000000000, bytes_accessed=200_000, transcendentals=0),
        name="repack",
    )(tail, after)


def paint(values, acc_ref, spill=False):
    slots = values.shape[1]
    cell = values[0:1].astype(jnp.int32)
    row = lax.shift_right_logical(cell, 13) * STRIDE + (lax.shift_right_logical(cell, 8) & 31)
    if spill:
        row = row - MAIN
    base_z = cell & 255
    next_z = (base_z + 1) & 255
    frac_x, frac_y, frac_z = values[1:2], values[2:3], values[3:4]
    rest_x, rest_y, rest_z = 1.0 - frac_x, 1.0 - frac_y, 1.0 - frac_z
    zero = jnp.zeros((), bf16)

    def short(value):
        return value.astype(f32).astype(bf16)

    count = 48 if spill else MAIN
    row_ids = short(lax.broadcasted_iota(jnp.int32, (count, slots), 0))
    corner = jnp.where(row_ids == short(row + STRIDE), short(frac_x * rest_y), zero)
    corner = jnp.where(row_ids == short(row + STRIDE + 1), short(frac_x * frac_y), corner)
    if not spill:
        corner = jnp.where(row_ids == short(row), short(rest_x * rest_y), corner)
        corner = jnp.where(row_ids == short(row + 1), short(rest_x * frac_y), corner)
    z_ids = short(lax.broadcasted_iota(jnp.int32, (NG, slots), 0))
    at_low, at_high = z_ids == short(base_z), z_ids == short(next_z)
    for i in range(3):
        weight = values[4 + i : 5 + i]
        line = jnp.where(at_low, short(weight * rest_z), zero)
        line = jnp.where(at_high, short(weight * frac_z), line)
        acc_ref[:count, i * NG : (i + 1) * NG] += lax.dot_general(
            corner, line, (((1,), (1,)), ((), ())), preferred_element_type=f32
        )


def near_kernel(held_ref, inner_ref, outer_ref, below2_ref, out_ref):
    out_ref[...] = jnp.zeros_like(out_ref)
    even = lax.axis_index("slab") % 2 == 0

    def body(step, carry):
        def group(ref, index):
            return ref[:, pl.ds(pl.multiple_of((3 * step + index) * CAP, CAP), CAP)]

        def pick(first, then, index):
            return jnp.where(even, group(first, index), group(then, index))

        paint(group(held_ref, 1), out_ref)
        paint(group(held_ref, 0), out_ref, spill=True)
        paint(pick(inner_ref, outer_ref, 0), out_ref)
        paint(pick(outer_ref, inner_ref, 2), out_ref)
        paint(pick(outer_ref, inner_ref, 1), out_ref, spill=True)
        paint(below2_ref[:, pl.ds(pl.multiple_of(step * CAP, CAP), CAP)], out_ref, spill=True)
        return carry

    lax.fori_loop(0, 3, body, 0)


def paint_near(held, inner, outer, below2):
    return pl.pallas_call(
        near_kernel,
        out_shape=jax.ShapeDtypeStruct((MAIN, 3 * NG), f32),
        in_specs=[VMEM] * 4,
        out_specs=VMEM,
        compiler_params=PARAMS,
        cost_estimate=pl.CostEstimate(flops=9059696640, bytes_accessed=2_000_000, transcendentals=0),
        name="paint_near",
    )(held, inner, outer, below2)


def tail_kernel(tail_ref, near_ref, plain_high, plain_low, scaled_high, scaled_low, out_ref, values, painted):
    for which in range(2):
        turned = tail_ref[:, 8 * which : 8 * which + 8, :].reshape(N_SLAB, 128).T
        for k in range(0, 16, 2):
            values[which, :, 64 * k : 64 * k + 128] = jnp.concatenate(
                [turned[8 * k : 8 * k + 8, :], turned[8 * k + 8 : 8 * k + 16, :]], axis=1
            )
    painted[...] = near_ref[...]
    paint(values[0], painted)
    paint(values[1], painted, spill=True)
    for i in range(3):
        data = painted[:, i * NG : (i + 1) * NG]
        high = data.astype(bf16)
        low = (data - high.astype(f32)).astype(bf16)
        table_high, table_low = (scaled_high, scaled_low) if i == 2 else (plain_high, plain_low)
        dot = functools.partial(jnp.dot, preferred_element_type=f32)
        result = dot(high, table_high[...]) + (dot(low, table_high[...]) + dot(high, table_low[...]))
        for part in range(2):
            block = 2 * i + part
            for p in range(N_PENCIL):
                at = part * NG + p * 32
                chunk = jnp.concatenate(
                    [result[x * STRIDE : (x + 1) * STRIDE, at : at + 32] for x in range(CX)], axis=1
                )
                out_ref[p, block * CY : (block + 1) * CY, :] = chunk[:CY]
                out_ref[p, 6 * CY + block : 6 * CY + block + 1, :] = chunk[CY : CY + 1]
    out_ref[:, 6 * CY + 6 :, :] = jnp.zeros((N_PENCIL, 2, 128), f32)


def paint_tail_transform_z(tail, near, plain, scaled):
    return pl.pallas_call(
        tail_kernel,
        out_shape=jax.ShapeDtypeStruct((N_PENCIL, CHUNK, 128), f32),
        in_specs=[VMEM] * 6,
        out_specs=VMEM,
        scratch_shapes=[pltpu.VMEM((2, 8, TAILS), f32), pltpu.VMEM((MAIN, 3 * NG), f32)],
        compiler_params=PARAMS,
        name="paint_tail_transform_z",
    )(tail, near, *plain, *scaled)


def mixed_rhs(real, imag):
    return jnp.concatenate(
        [jnp.concatenate([real, imag], axis=1), jnp.concatenate([imag, -real], axis=1)], axis=0
    )


def y_kernel(in_ref, table_high, table_low, out_ref):
    first = lax.broadcasted_iota(jnp.int32, (CY, 128), 0) == 0
    blocks = []
    for block in range(6):
        parts = []
        for src in range(N_PENCIL):
            spilled = in_ref[(src - 1) % N_PENCIL, 6 * CY + block : 6 * CY + block + 1, :]
            parts.append(in_ref[src, block * CY : (block + 1) * CY, :] + jnp.where(first, spilled, 0.0))
        blocks.append(jnp.concatenate(parts, axis=0))
    field = product(table_high[:, 2 * NG :], table_low[:, 2 * NG :], mixed_rhs(blocks[0], blocks[1]))
    sides = jnp.concatenate([mixed_rhs(blocks[2], blocks[3]), mixed_rhs(blocks[4], blocks[5])], axis=0)
    mixed = product(table_high[...], table_low[...], sides)
    for f, result in enumerate((field, mixed)):
        for part in range(2):
            for x in range(CX):
                at = part * 128 + x * 32
                chunk = jnp.concatenate(
                    [result[r * N_SLAB : (r + 1) * N_SLAB, at : at + 32] for r in range(4)], axis=1
                )
                out_ref[pl.ds(x * 4 + f * 2 + part, N_SLAB, stride=16), :] = chunk


def transform_y(by_rows, table):
    return pl.pallas_call(
        y_kernel,
        out_shape=jax.ShapeDtypeStruct((N_SLAB * 16, 128), f32),
        in_specs=[VMEM] * 3,
        out_specs=VMEM,
        compiler_params=PARAMS,
        name="transform_y",
    )(by_rows, *table)


def wavenumber(position):
    return jnp.where(position < NG // 2, position, position - NG).astype(f32)


def x_kernel(in_ref, table_high, table_low, out_ref):
    lines = [in_ref[pl.ds(block, NG, stride=4), :] for block in range(4)]
    data = jnp.concatenate([mixed_rhs(lines[0], lines[1]), mixed_rhs(lines[2], lines[3])], axis=0)
    mixed = product(table_high[...], table_low[...], data)
    lane = lax.broadcasted_iota(jnp.int32, (1, 128), 1)
    wave_y = wavenumber(lax.axis_index("slab") * 4 + lane // 32)
    wave_z = wavenumber(lax.axis_index("pencil") * 32 + lane % 32)
    wave_x = wavenumber(lax.broadcasted_iota(jnp.int32, (NG, 1), 0))
    wave_sq = wave_x * wave_x + wave_y * wave_y + wave_z * wave_z
    factor = jnp.where(wave_sq > 0, out_scale / jnp.sqrt(jnp.maximum(wave_sq, 1.0)), 0.0) / NG**1.5
    out_ref[0] = (mixed[:, 128:] * factor).T
    out_ref[1] = (mixed[:, :128] * -factor).T


def transform_x(by_cols, table):
    return pl.pallas_call(
        x_kernel,
        out_shape=jax.ShapeDtypeStruct((2, 128, NG), f32),
        in_specs=[VMEM] * 3,
        out_specs=VMEM,
        compiler_params=PARAMS,
        name="transform_x",
    )(by_cols, *table)


def local(cells, fractions, adjoint_pos, adjoint_vel, counts):
    plain, scaled, table_y, table_x = [tuple(jnp.asarray(t) for t in pair) for pair in host_tables()]
    arrays = (counts, cells, fractions, adjoint_pos, adjoint_vel)
    tail, to_left, mid, to_right = pack(*arrays)
    from_right = shifted(to_left, "pencil", -1)
    from_left = shifted(to_right, "pencil", 1)
    columns = (from_left, mid, from_right)
    held = jnp.concatenate(columns, axis=1)
    inner = swapped(held, 0)
    outer = swapped(held, 1)
    from_below2 = shifted(jnp.concatenate([held[:, (3 * c + 2) * CAP : (3 * c + 3) * CAP] for c in range(3)], axis=1), "slab", 2)
    tail = lax.all_to_all(tail.reshape(N_SLAB, 2, 128), "slab", 0, 0, tiled=True)
    tail = lax.all_to_all(repack(tail.reshape(2 * N_SLAB, 128), from_below2), "pencil", 0, 0, tiled=True)
    near = paint_near(held, inner, outer, from_below2)
    by_rows = paint_tail_transform_z(tail, near, plain, scaled)
    by_rows = lax.all_to_all(by_rows, "pencil", 0, 0, tiled=True)
    by_cols = transform_y(by_rows, table_y)
    by_cols = lax.all_to_all(by_cols.reshape(N_SLAB, 16, 128), "slab", 0, 0, tiled=True)
    result = transform_x(by_cols.reshape(N_SLAB * 16, 128), table_x)
    return result.reshape(2, CX, 32, NG)


def solution(mesh):
    in_specs = (
        P(("slab", "pencil"), None),
        P(None, ("slab", "pencil"), None),
        P(None, ("slab", "pencil"), None),
        P(None, ("slab", "pencil"), None),
        P(("slab", "pencil"), None),
    )
    out_specs = P(None, "slab", "pencil", None)
    return jax.shard_map(local, mesh=mesh, in_specs=in_specs, out_specs=out_specs, check_vma=False)
```

```python
import functools

import jax
import jax.numpy as jnp
import ml_dtypes
import numpy as np
from jax import lax
from jax.experimental import pallas as pl
from jax.experimental.pallas import tpu as pltpu
from jax.sharding import PartitionSpec as P

NG = 256
CAP = 512
TAIL = 2
N_SLAB = 64
N_PENCIL = 8
OWNERS = 512
NEAR = 9 * CAP
TAILS = OWNERS * TAIL
CX = 4
CY = 32
STRIDE = 40
MAIN = CX * STRIDE
CHUNK = 6 * CY + 8

kick_factor = 0.8
drift_factor = 1.25
out_scale = 3.0

f32 = jnp.float32
bf16 = jnp.bfloat16
VMEM = pl.BlockSpec(memory_space=pltpu.VMEM)
SMEM = pl.BlockSpec(memory_space=pltpu.SMEM)
HBM = pl.BlockSpec(memory_space=pltpu.HBM)
ANY = pl.BlockSpec(memory_space=pl.ANY)
WIDE = pltpu.CompilerParams(vmem_limit_bytes=60 * 1024 * 1024)
PARAMS = pltpu.CompilerParams(vmem_limit_bytes=24 * 1024 * 1024)


def split_table(table):
    high = table.astype(ml_dtypes.bfloat16)
    low = (table - high.astype(np.float64)).astype(ml_dtypes.bfloat16)
    return high, low


@functools.cache
def host_tables():
    idx = np.arange(NG)
    angles = (idx[:, None] * idx[None, :] % NG) * (2.0 * np.pi / NG)
    cosine, sine = np.cos(angles), np.sin(angles)
    wave = np.where(idx < NG // 2, idx, idx - NG).astype(np.float64)
    table_z = np.concatenate([cosine, -sine], axis=1)
    table_kz = np.concatenate([cosine * wave[None, :], -sine * wave[None, :]], axis=1)
    table_k = np.concatenate([cosine * wave[:, None], sine * wave[:, None], cosine, sine], axis=1)
    order = np.array([4 * s + r for r in range(4) for s in range(N_SLAB)])
    return (
        split_table(table_z),
        split_table(table_kz),
        split_table(table_k[order]),
        split_table(table_k),
    )


def swapped(block, first):
    count = lax.axis_size("slab")
    pairs = [((i + first) % count, (i + first + 1) % count) for i in range(0, count, 2)]
    return lax.ppermute(block, "slab", pairs + [(b, a) for a, b in pairs])


def shifted(block, axis, distance):
    devices = range(lax.axis_size(axis))
    route = [((i - distance) % len(devices), i) for i in devices]
    return lax.ppermute(block, axis, route)


def product(table_high, table_low, data):
    high = data.astype(bf16)
    low = (data - high.astype(f32)).astype(bf16)
    dot = functools.partial(jnp.dot, preferred_element_type=f32)
    return dot(table_high, high) + (dot(table_high, low) + dot(table_low, high))


def start_copies(pairs, sems):
    copies = [pltpu.make_async_copy(src, dst, sems.at[i]) for i, (src, dst) in enumerate(pairs)]
    for copy in copies:
        copy.start()
    return copies


def particle_rows(out, lanes, live, cells, frac, pos, vel):
    out[0:1, lanes] = cells.astype(f32)
    for i in range(3):
        out[1 + i : 2 + i, lanes] = frac[i]
        weight = kick_factor * (vel[i] + drift_factor * pos[i])
        out[4 + i : 5 + i, lanes] = jnp.where(live, weight, 0.0)
    out[7:8, lanes] = jnp.zeros(cells.shape, f32)


def pack_kernel(counts_hbm, cells_hbm, frac_hbm, pos_hbm, vel_hbm, tail_ref, left_ref, mid_ref, right_ref, counts_ref, cells_ref, frac_ref, pos_ref, vel_ref, counts_smem, rows, columns, flat, sems):
    copies = start_copies(
        [(counts_hbm, counts_ref), (counts_hbm, counts_smem), (cells_hbm, cells_ref), (frac_hbm, frac_ref), (pos_hbm, pos_ref), (vel_hbm, vel_ref)], sems
    )
    width = counts_ref.shape[1]
    slot_of = lax.broadcasted_iota(jnp.int32, (width, TAILS), 1)
    entry = lax.broadcasted_iota(jnp.int32, (width, TAILS), 0)
    spread = jnp.where(slot_of // TAIL + 9 == entry, 1.0, 0.0).astype(bf16)
    for copy in copies:
        copy.wait()

    def fill(out, lanes, src, live):
        particle_rows(out, lanes, live, cells_ref[:, src], frac_ref[:, :, src], pos_ref[:, :, src], vel_ref[:, :, src])

    counts = jnp.broadcast_to(counts_ref[...].astype(f32), (8, width)).astype(bf16)
    tail_count = jnp.dot(counts, spread, preferred_element_type=f32)[0:1]
    live = (lax.broadcasted_iota(jnp.int32, (1, TAILS), 1) % TAIL).astype(f32) < tail_count
    fill(rows, pl.ds(0, TAILS), pl.ds(NEAR, TAILS), live)
    columns[...] = rows[...].T
    for k in range(16):
        flat[:, 8 * k : 8 * k + 8] = columns[pl.ds(k, N_SLAB, stride=16), :]
    tail_ref[pl.ds(0, N_SLAB, stride=2), :] = flat[...]
    tail_ref[pl.ds(1, N_SLAB, stride=2), :] = jnp.concatenate([flat[N_SLAB - 1 :], flat[: N_SLAB - 1]], axis=0)
    for group in range(9):
        live = lax.broadcasted_iota(jnp.int32, (1, CAP), 1) < counts_smem[0, group]
        fill((left_ref, mid_ref, right_ref)[group % 3], pl.ds(group // 3 * CAP, CAP), pl.ds(group * CAP, CAP), live)


def pack(counts, cells, fractions, adjoint_pos, adjoint_vel):
    field = pltpu.VMEM(fractions.shape, f32)
    side = jax.ShapeDtypeStruct((8, 3 * CAP), f32)
    return pl.pallas_call(
        pack_kernel,
        out_shape=(jax.ShapeDtypeStruct((2 * N_SLAB, 128), f32), side, side, side),
        in_specs=[HBM] * 5,
        out_specs=(VMEM,) * 4,
        scratch_shapes=[
            pltpu.VMEM(counts.shape, jnp.int32),
            pltpu.VMEM(cells.shape, jnp.int32),
            field,
            field,
            field,
            pltpu.SMEM(counts.shape, jnp.int32),
            pltpu.VMEM((8, TAILS), f32),
            pltpu.VMEM((TAILS, 8), f32),
            pltpu.VMEM((N_SLAB, 128), f32),
            pltpu.SemaphoreType.DMA((6,)),
        ],
        compiler_params=WIDE,
        name="pack",
    )(counts, cells, fractions, adjoint_pos, adjoint_vel)


def repack_kernel(in_ref, after_ref, out_ref):
    for which in range(2):
        rows = in_ref[pl.ds(which, N_SLAB, stride=2), :]
        for p in range(N_PENCIL):
            for k in range(8):
                out_ref[p, 8 * which : 8 * which + 8, 16 * k : 16 * k + 16] = rows[8 * k : 8 * k + 8, 16 * p : 16 * p + 16]


def repack(tail, after):
    return pl.pallas_call(
        repack_kernel,
        out_shape=jax.ShapeDtypeStruct((N_PENCIL, 16, 128), f32),
        in_specs=[VMEM, ANY],
        out_specs=VMEM,
        compiler_params=PARAMS,
        cost_estimate=pl.CostEstimate(flops=3000000000, bytes_accessed=200_000, transcendentals=0),
        name="repack",
    )(tail, after)


def paint(values, acc_ref, spill=False):
    slots = values.shape[1]
    cell = values[0:1].astype(jnp.int32)
    row = lax.shift_right_logical(cell, 13) * STRIDE + (lax.shift_right_logical(cell, 8) & 31)
    if spill:
        row = row - MAIN
    base_z = cell & 255
    next_z = (base_z + 1) & 255
    frac_x, frac_y, frac_z = values[1:2], values[2:3], values[3:4]
    rest_x, rest_y, rest_z = 1.0 - frac_x, 1.0 - frac_y, 1.0 - frac_z
    zero = jnp.zeros((), bf16)

    def short(value):
        return value.astype(f32).astype(bf16)

    count = 48 if spill else MAIN
    row_ids = short(lax.broadcasted_iota(jnp.int32, (count, slots), 0))
    corner = jnp.where(row_ids == short(row + STRIDE), short(frac_x * rest_y), zero)
    corner = jnp.where(row_ids == short(row + STRIDE + 1), short(frac_x * frac_y), corner)
    if not spill:
        corner = jnp.where(row_ids == short(row), short(rest_x * rest_y), corner)
        corner = jnp.where(row_ids == short(row + 1), short(rest_x * frac_y), corner)
    z_ids = short(lax.broadcasted_iota(jnp.int32, (NG, slots), 0))
    at_low, at_high = z_ids == short(base_z), z_ids == short(next_z)
    for i in range(3):
        weight = values[4 + i : 5 + i]
        line = jnp.where(at_low, short(weight * rest_z), zero)
        line = jnp.where(at_high, short(weight * frac_z), line)
        acc_ref[:count, i * NG : (i + 1) * NG] += lax.dot_general(
            corner, line, (((1,), (1,)), ((), ())), preferred_element_type=f32
        )


def held_kernel(held_ref, after_ref, out_ref):
    out_ref[...] = jnp.zeros_like(out_ref)
    for step in range(3):
        paint(held_ref[:, (3 * step + 1) * CAP : (3 * step + 2) * CAP], out_ref)
        paint(held_ref[:, 3 * step * CAP : (3 * step + 1) * CAP], out_ref, spill=True)


def paint_held(held, after):
    return pl.pallas_call(
        held_kernel,
        out_shape=jax.ShapeDtypeStruct((MAIN, 3 * NG), f32),
        in_specs=[VMEM, ANY],
        out_specs=VMEM,
        compiler_params=PARAMS,
        cost_estimate=pl.CostEstimate(flops=1_000_000_000, bytes_accessed=1_000_000, transcendentals=0),
        name="paint_held",
    )(held, after)


def near_kernel(first_ref, inner_ref, outer_ref, below2_ref, out_ref):
    out_ref[...] = first_ref[...]
    even = lax.axis_index("slab") % 2 == 0

    def body(step, carry):
        def group(ref, index):
            return ref[:, pl.ds(pl.multiple_of((3 * step + index) * CAP, CAP), CAP)]

        def pick(first, then, index):
            return jnp.where(even, group(first, index), group(then, index))

        paint(pick(inner_ref, outer_ref, 0), out_ref)
        paint(pick(outer_ref, inner_ref, 2), out_ref)
        paint(pick(outer_ref, inner_ref, 1), out_ref, spill=True)
        paint(below2_ref[:, pl.ds(pl.multiple_of(step * CAP, CAP), CAP)], out_ref, spill=True)
        return carry

    lax.fori_loop(0, 3, body, 0)


def paint_near(first, inner, outer, below2):
    return pl.pallas_call(
        near_kernel,
        out_shape=jax.ShapeDtypeStruct((MAIN, 3 * NG), f32),
        in_specs=[VMEM] * 4,
        out_specs=VMEM,
        compiler_params=PARAMS,
        cost_estimate=pl.CostEstimate(flops=4 * NEAR * MAIN * 3 * NG, bytes_accessed=2_000_000, transcendentals=0),
        name="paint_near",
    )(first, inner, outer, below2)


def tail_kernel(tail_ref, near_ref, plain_high, plain_low, scaled_high, scaled_low, out_ref, values, painted):
    for which in range(2):
        turned = tail_ref[:, 8 * which : 8 * which + 8, :].reshape(N_SLAB, 128).T
        for k in range(0, 16, 2):
            values[which, :, 64 * k : 64 * k + 128] = jnp.concatenate(
                [turned[8 * k : 8 * k + 8, :], turned[8 * k + 8 : 8 * k + 16, :]], axis=1
            )
    painted[...] = near_ref[...]
    paint(values[0], painted)
    paint(values[1], painted, spill=True)
    for i in range(3):
        data = painted[:, i * NG : (i + 1) * NG]
        high = data.astype(bf16)
        low = (data - high.astype(f32)).astype(bf16)
        table_high, table_low = (scaled_high, scaled_low) if i == 2 else (plain_high, plain_low)
        dot = functools.partial(jnp.dot, preferred_element_type=f32)
        result = dot(high, table_high[...]) + (dot(low, table_high[...]) + dot(high, table_low[...]))
        for part in range(2):
            block = 2 * i + part
            for p in range(N_PENCIL):
                at = part * NG + p * 32
                chunk = jnp.concatenate(
                    [result[x * STRIDE : (x + 1) * STRIDE, at : at + 32] for x in range(CX)], axis=1
                )
                out_ref[p, block * CY : (block + 1) * CY, :] = chunk[:CY]
                out_ref[p, 6 * CY + block : 6 * CY + block + 1, :] = chunk[CY : CY + 1]
    out_ref[:, 6 * CY + 6 :, :] = jnp.zeros((N_PENCIL, 2, 128), f32)


def paint_tail_transform_z(tail, near, plain, scaled):
    return pl.pallas_call(
        tail_kernel,
        out_shape=jax.ShapeDtypeStruct((N_PENCIL, CHUNK, 128), f32),
        in_specs=[VMEM] * 6,
        out_specs=VMEM,
        scratch_shapes=[pltpu.VMEM((2, 8, TAILS), f32), pltpu.VMEM((MAIN, 3 * NG), f32)],
        compiler_params=PARAMS,
        name="paint_tail_transform_z",
    )(tail, near, *plain, *scaled)


def mixed_rhs(real, imag):
    return jnp.concatenate(
        [jnp.concatenate([real, imag], axis=1), jnp.concatenate([imag, -real], axis=1)], axis=0
    )


def y_kernel(in_ref, table_high, table_low, out_ref):
    first = lax.broadcasted_iota(jnp.int32, (CY, 128), 0) == 0
    blocks = []
    for block in range(6):
        parts = []
        for src in range(N_PENCIL):
            spilled = in_ref[(src - 1) % N_PENCIL, 6 * CY + block : 6 * CY + block + 1, :]
            parts.append(in_ref[src, block * CY : (block + 1) * CY, :] + jnp.where(first, spilled, 0.0))
        blocks.append(jnp.concatenate(parts, axis=0))
    field = product(table_high[:, 2 * NG :], table_low[:, 2 * NG :], mixed_rhs(blocks[0], blocks[1]))
    sides = jnp.concatenate([mixed_rhs(blocks[2], blocks[3]), mixed_rhs(blocks[4], blocks[5])], axis=0)
    mixed = product(table_high[...], table_low[...], sides)
    for f, result in enumerate((field, mixed)):
        for part in range(2):
            for x in range(CX):
                at = part * 128 + x * 32
                chunk = jnp.concatenate(
                    [result[r * N_SLAB : (r + 1) * N_SLAB, at : at + 32] for r in range(4)], axis=1
                )
                out_ref[pl.ds(x * 4 + f * 2 + part, N_SLAB, stride=16), :] = chunk


def transform_y(by_rows, table):
    return pl.pallas_call(
        y_kernel,
        out_shape=jax.ShapeDtypeStruct((N_SLAB * 16, 128), f32),
        in_specs=[VMEM] * 3,
        out_specs=VMEM,
        compiler_params=PARAMS,
        name="transform_y",
    )(by_rows, *table)


def wavenumber(position):
    return jnp.where(position < NG // 2, position, position - NG).astype(f32)


def x_kernel(in_ref, table_high, table_low, out_ref):
    lines = [in_ref[pl.ds(block, NG, stride=4), :] for block in range(4)]
    data = jnp.concatenate([mixed_rhs(lines[0], lines[1]), mixed_rhs(lines[2], lines[3])], axis=0)
    mixed = product(table_high[...], table_low[...], data)
    lane = lax.broadcasted_iota(jnp.int32, (1, 128), 1)
    wave_y = wavenumber(lax.axis_index("slab") * 4 + lane // 32)
    wave_z = wavenumber(lax.axis_index("pencil") * 32 + lane % 32)
    wave_x = wavenumber(lax.broadcasted_iota(jnp.int32, (NG, 1), 0))
    wave_sq = wave_x * wave_x + wave_y * wave_y + wave_z * wave_z
    factor = jnp.where(wave_sq > 0, out_scale / jnp.sqrt(jnp.maximum(wave_sq, 1.0)), 0.0) / NG**1.5
    out_ref[0] = (mixed[:, 128:] * factor).T
    out_ref[1] = (mixed[:, :128] * -factor).T


def transform_x(by_cols, table):
    return pl.pallas_call(
        x_kernel,
        out_shape=jax.ShapeDtypeStruct((2, 128, NG), f32),
        in_specs=[VMEM] * 3,
        out_specs=VMEM,
        compiler_params=PARAMS,
        name="transform_x",
    )(by_cols, *table)


def local(cells, fractions, adjoint_pos, adjoint_vel, counts):
    plain, scaled, table_y, table_x = [tuple(jnp.asarray(t) for t in pair) for pair in host_tables()]
    arrays = (counts, cells, fractions, adjoint_pos, adjoint_vel)
    tail, to_left, mid, to_right = pack(*arrays)
    from_right = shifted(to_left, "pencil", -1)
    from_left = shifted(to_right, "pencil", 1)
    columns = (from_left, mid, from_right)
    held = jnp.concatenate(columns, axis=1)
    inner = swapped(held, 0)
    outer = swapped(held, 1)
    from_below2 = shifted(jnp.concatenate([held[:, (3 * c + 2) * CAP : (3 * c + 3) * CAP] for c in range(3)], axis=1), "slab", 2)
    tail = lax.all_to_all(tail.reshape(N_SLAB, 2, 128), "slab", 0, 0, tiled=True)
    first = paint_held(held, from_below2)
    tail = lax.all_to_all(repack(tail.reshape(2 * N_SLAB, 128), first), "pencil", 0, 0, tiled=True)
    near = paint_near(first, inner, outer, from_below2)
    by_rows = paint_tail_transform_z(tail, near, plain, scaled)
    by_rows = lax.all_to_all(by_rows, "pencil", 0, 0, tiled=True)
    by_cols = transform_y(by_rows, table_y)
    by_cols = lax.all_to_all(by_cols.reshape(N_SLAB, 16, 128), "slab", 0, 0, tiled=True)
    result = transform_x(by_cols.reshape(N_SLAB * 16, 128), table_x)
    return result.reshape(2, CX, 32, NG)


def solution(mesh):
    in_specs = (
        P(("slab", "pencil"), None),
        P(None, ("slab", "pencil"), None),
        P(None, ("slab", "pencil"), None),
        P(None, ("slab", "pencil"), None),
        P(("slab", "pencil"), None),
    )
    out_specs = P(None, "slab", "pencil", None)
    return jax.shard_map(local, mesh=mesh, in_specs=in_specs, out_specs=out_specs, check_vma=False)
```

```python
import functools

import jax
import jax.numpy as jnp
import ml_dtypes
import numpy as np
from jax import lax
from jax.experimental import pallas as pl
from jax.experimental.pallas import tpu as pltpu
from jax.sharding import PartitionSpec as P

NG = 256
CAP = 512
TAIL = 2
N_SLAB = 64
N_PENCIL = 8
OWNERS = 512
NEAR = 9 * CAP
TAILS = OWNERS * TAIL
CX = 4
CY = 32
STRIDE = 40
MAIN = CX * STRIDE
CHUNK = 6 * CY + 8

kick_factor = 0.8
drift_factor = 1.25
out_scale = 3.0

f32 = jnp.float32
bf16 = jnp.bfloat16
VMEM = pl.BlockSpec(memory_space=pltpu.VMEM)
SMEM = pl.BlockSpec(memory_space=pltpu.SMEM)
HBM = pl.BlockSpec(memory_space=pltpu.HBM)
ANY = pl.BlockSpec(memory_space=pl.ANY)
WIDE = pltpu.CompilerParams(vmem_limit_bytes=60 * 1024 * 1024)
PARAMS = pltpu.CompilerParams(vmem_limit_bytes=24 * 1024 * 1024)


def split_table(table):
    high = table.astype(ml_dtypes.bfloat16)
    low = (table - high.astype(np.float64)).astype(ml_dtypes.bfloat16)
    return high, low


@functools.cache
def host_tables():
    idx = np.arange(NG)
    angles = (idx[:, None] * idx[None, :] % NG) * (2.0 * np.pi / NG)
    cosine, sine = np.cos(angles), np.sin(angles)
    wave = np.where(idx < NG // 2, idx, idx - NG).astype(np.float64)
    table_z = np.concatenate([cosine, -sine], axis=1)
    table_kz = np.concatenate([cosine * wave[None, :], -sine * wave[None, :]], axis=1)
    table_k = np.concatenate([cosine * wave[:, None], sine * wave[:, None], cosine, sine], axis=1)
    order = np.array([4 * s + r for r in range(4) for s in range(N_SLAB)])
    return (
        split_table(table_z),
        split_table(table_kz),
        split_table(table_k[order]),
        split_table(table_k),
    )


def swapped(block, first):
    count = lax.axis_size("slab")
    pairs = [((i + first) % count, (i + first + 1) % count) for i in range(0, count, 2)]
    return lax.ppermute(block, "slab", pairs + [(b, a) for a, b in pairs])


def shifted(block, axis, distance):
    devices = range(lax.axis_size(axis))
    route = [((i - distance) % len(devices), i) for i in devices]
    return lax.ppermute(block, axis, route)


def product(table_high, table_low, data):
    high = data.astype(bf16)
    low = (data - high.astype(f32)).astype(bf16)
    dot = functools.partial(jnp.dot, preferred_element_type=f32)
    return dot(table_high, high) + (dot(table_high, low) + dot(table_low, high))


def start_copies(pairs, sems):
    copies = [pltpu.make_async_copy(src, dst, sems.at[i]) for i, (src, dst) in enumerate(pairs)]
    for copy in copies:
        copy.start()
    return copies


def particle_rows(out, lanes, live, cells, frac, pos, vel):
    out[0:1, lanes] = cells.astype(f32)
    for i in range(3):
        out[1 + i : 2 + i, lanes] = frac[i]
        weight = kick_factor * (vel[i] + drift_factor * pos[i])
        out[4 + i : 5 + i, lanes] = jnp.where(live, weight, 0.0)
    out[7:8, lanes] = jnp.zeros(cells.shape, f32)


def pack_kernel(counts_hbm, cells_hbm, frac_hbm, pos_hbm, vel_hbm, tail_ref, left_ref, mid_ref, right_ref, counts_ref, cells_ref, frac_ref, pos_ref, vel_ref, counts_smem, rows, columns, flat, sems):
    copies = start_copies(
        [(counts_hbm, counts_ref), (counts_hbm, counts_smem), (cells_hbm, cells_ref), (frac_hbm, frac_ref), (pos_hbm, pos_ref), (vel_hbm, vel_ref)], sems
    )
    width = counts_ref.shape[1]
    slot_of = lax.broadcasted_iota(jnp.int32, (width, TAILS), 1)
    entry = lax.broadcasted_iota(jnp.int32, (width, TAILS), 0)
    spread = jnp.where(slot_of // TAIL + 9 == entry, 1.0, 0.0).astype(bf16)
    for copy in copies:
        copy.wait()

    def fill(out, lanes, src, live):
        particle_rows(out, lanes, live, cells_ref[:, src], frac_ref[:, :, src], pos_ref[:, :, src], vel_ref[:, :, src])

    counts = jnp.broadcast_to(counts_ref[...].astype(f32), (8, width)).astype(bf16)
    tail_count = jnp.dot(counts, spread, preferred_element_type=f32)[0:1]
    live = (lax.broadcasted_iota(jnp.int32, (1, TAILS), 1) % TAIL).astype(f32) < tail_count
    fill(rows, pl.ds(0, TAILS), pl.ds(NEAR, TAILS), live)
    columns[...] = rows[...].T
    for k in range(16):
        flat[:, 8 * k : 8 * k + 8] = columns[pl.ds(k, N_SLAB, stride=16), :]
    for p in range(N_PENCIL):
        for k in range(8):
            tail_ref[p, :, 16 * k : 16 * k + 16] = flat[8 * k : 8 * k + 8, 16 * p : 16 * p + 16]
    for group in range(9):
        live = lax.broadcasted_iota(jnp.int32, (1, CAP), 1) < counts_smem[0, group]
        fill((left_ref, mid_ref, right_ref)[group % 3], pl.ds(group // 3 * CAP, CAP), pl.ds(group * CAP, CAP), live)


def pack(counts, cells, fractions, adjoint_pos, adjoint_vel):
    field = pltpu.VMEM(fractions.shape, f32)
    side = jax.ShapeDtypeStruct((8, 3 * CAP), f32)
    return pl.pallas_call(
        pack_kernel,
        out_shape=(jax.ShapeDtypeStruct((N_PENCIL, 8, 128), f32), side, side, side),
        in_specs=[HBM] * 5,
        out_specs=(VMEM,) * 4,
        scratch_shapes=[
            pltpu.VMEM(counts.shape, jnp.int32),
            pltpu.VMEM(cells.shape, jnp.int32),
            field,
            field,
            field,
            pltpu.SMEM(counts.shape, jnp.int32),
            pltpu.VMEM((8, TAILS), f32),
            pltpu.VMEM((TAILS, 8), f32),
            pltpu.VMEM((N_SLAB, 128), f32),
            pltpu.SemaphoreType.DMA((6,)),
        ],
        compiler_params=WIDE,
        name="pack",
    )(counts, cells, fractions, adjoint_pos, adjoint_vel)


def repack_kernel(in_ref, after_ref, out_ref, flat):
    for p in range(N_PENCIL):
        for k in range(8):
            flat[8 * k : 8 * k + 8, 16 * p : 16 * p + 16] = in_ref[p, :, 16 * k : 16 * k + 16]
    out_ref[pl.ds(0, N_SLAB, stride=2), :] = flat[...]
    out_ref[pl.ds(1, N_SLAB, stride=2), :] = jnp.concatenate([flat[N_SLAB - 1 :], flat[: N_SLAB - 1]], axis=0)


def repack(tail, after):
    return pl.pallas_call(
        repack_kernel,
        out_shape=jax.ShapeDtypeStruct((2 * N_SLAB, 128), f32),
        in_specs=[VMEM, ANY],
        out_specs=VMEM,
        scratch_shapes=[pltpu.VMEM((N_SLAB, 128), f32)],
        compiler_params=PARAMS,
        cost_estimate=pl.CostEstimate(flops=3000000000, bytes_accessed=200_000, transcendentals=0),
        name="repack",
    )(tail, after)


def paint(values, acc_ref, spill=False):
    slots = values.shape[1]
    cell = values[0:1].astype(jnp.int32)
    row = lax.shift_right_logical(cell, 13) * STRIDE + (lax.shift_right_logical(cell, 8) & 31)
    if spill:
        row = row - MAIN
    base_z = cell & 255
    next_z = (base_z + 1) & 255
    frac_x, frac_y, frac_z = values[1:2], values[2:3], values[3:4]
    rest_x, rest_y, rest_z = 1.0 - frac_x, 1.0 - frac_y, 1.0 - frac_z
    zero = jnp.zeros((), bf16)

    def short(value):
        return value.astype(f32).astype(bf16)

    count = 48 if spill else MAIN
    row_ids = short(lax.broadcasted_iota(jnp.int32, (count, slots), 0))
    corner = jnp.where(row_ids == short(row + STRIDE), short(frac_x * rest_y), zero)
    corner = jnp.where(row_ids == short(row + STRIDE + 1), short(frac_x * frac_y), corner)
    if not spill:
        corner = jnp.where(row_ids == short(row), short(rest_x * rest_y), corner)
        corner = jnp.where(row_ids == short(row + 1), short(rest_x * frac_y), corner)
    z_ids = short(lax.broadcasted_iota(jnp.int32, (NG, slots), 0))
    at_low, at_high = z_ids == short(base_z), z_ids == short(next_z)
    for i in range(3):
        weight = values[4 + i : 5 + i]
        line = jnp.where(at_low, short(weight * rest_z), zero)
        line = jnp.where(at_high, short(weight * frac_z), line)
        acc_ref[:count, i * NG : (i + 1) * NG] += lax.dot_general(
            corner, line, (((1,), (1,)), ((), ())), preferred_element_type=f32
        )


def near_kernel(held_ref, inner_ref, outer_ref, below2_ref, out_ref):
    out_ref[...] = jnp.zeros_like(out_ref)
    even = lax.axis_index("slab") % 2 == 0

    def body(step, carry):
        def group(ref, index):
            return ref[:, pl.ds(pl.multiple_of((3 * step + index) * CAP, CAP), CAP)]

        def pick(first, then, index):
            return jnp.where(even, group(first, index), group(then, index))

        paint(group(held_ref, 1), out_ref)
        paint(group(held_ref, 0), out_ref, spill=True)
        paint(pick(inner_ref, outer_ref, 0), out_ref)
        paint(pick(outer_ref, inner_ref, 2), out_ref)
        paint(pick(outer_ref, inner_ref, 1), out_ref, spill=True)
        paint(below2_ref[:, pl.ds(pl.multiple_of(step * CAP, CAP), CAP)], out_ref, spill=True)
        return carry

    lax.fori_loop(0, 3, body, 0)


def paint_near(held, inner, outer, below2):
    return pl.pallas_call(
        near_kernel,
        out_shape=jax.ShapeDtypeStruct((MAIN, 3 * NG), f32),
        in_specs=[VMEM] * 4,
        out_specs=VMEM,
        compiler_params=PARAMS,
        cost_estimate=pl.CostEstimate(flops=9059696640, bytes_accessed=2_000_000, transcendentals=0),
        name="paint_near",
    )(held, inner, outer, below2)


def tail_kernel(tail_ref, near_ref, plain_high, plain_low, scaled_high, scaled_low, out_ref, values, painted):
    for which in range(2):
        turned = tail_ref[pl.ds(which, N_SLAB, stride=2), :].T
        for k in range(0, 16, 2):
            values[which, :, 64 * k : 64 * k + 128] = jnp.concatenate(
                [turned[8 * k : 8 * k + 8, :], turned[8 * k + 8 : 8 * k + 16, :]], axis=1
            )
    painted[...] = near_ref[...]
    paint(values[0], painted)
    paint(values[1], painted, spill=True)
    for i in range(3):
        data = painted[:, i * NG : (i + 1) * NG]
        high = data.astype(bf16)
        low = (data - high.astype(f32)).astype(bf16)
        table_high, table_low = (scaled_high, scaled_low) if i == 2 else (plain_high, plain_low)
        dot = functools.partial(jnp.dot, preferred_element_type=f32)
        result = dot(high, table_high[...]) + (dot(low, table_high[...]) + dot(high, table_low[...]))
        for part in range(2):
            block = 2 * i + part
            for p in range(N_PENCIL):
                at = part * NG + p * 32
                chunk = jnp.concatenate(
                    [result[x * STRIDE : (x + 1) * STRIDE, at : at + 32] for x in range(CX)], axis=1
                )
                out_ref[p, block * CY : (block + 1) * CY, :] = chunk[:CY]
                out_ref[p, 6 * CY + block : 6 * CY + block + 1, :] = chunk[CY : CY + 1]
    out_ref[:, 6 * CY + 6 :, :] = jnp.zeros((N_PENCIL, 2, 128), f32)


def paint_tail_transform_z(tail, near, plain, scaled):
    return pl.pallas_call(
        tail_kernel,
        out_shape=jax.ShapeDtypeStruct((N_PENCIL, CHUNK, 128), f32),
        in_specs=[VMEM] * 6,
        out_specs=VMEM,
        scratch_shapes=[pltpu.VMEM((2, 8, TAILS), f32), pltpu.VMEM((MAIN, 3 * NG), f32)],
        compiler_params=PARAMS,
        name="paint_tail_transform_z",
    )(tail, near, *plain, *scaled)


def mixed_rhs(real, imag):
    return jnp.concatenate(
        [jnp.concatenate([real, imag], axis=1), jnp.concatenate([imag, -real], axis=1)], axis=0
    )


def y_kernel(in_ref, table_high, table_low, out_ref):
    first = lax.broadcasted_iota(jnp.int32, (CY, 128), 0) == 0
    blocks = []
    for block in range(6):
        parts = []
        for src in range(N_PENCIL):
            spilled = in_ref[(src - 1) % N_PENCIL, 6 * CY + block : 6 * CY + block + 1, :]
            parts.append(in_ref[src, block * CY : (block + 1) * CY, :] + jnp.where(first, spilled, 0.0))
        blocks.append(jnp.concatenate(parts, axis=0))
    field = product(table_high[:, 2 * NG :], table_low[:, 2 * NG :], mixed_rhs(blocks[0], blocks[1]))
    sides = jnp.concatenate([mixed_rhs(blocks[2], blocks[3]), mixed_rhs(blocks[4], blocks[5])], axis=0)
    mixed = product(table_high[...], table_low[...], sides)
    for f, result in enumerate((field, mixed)):
        for part in range(2):
            for x in range(CX):
                at = part * 128 + x * 32
                chunk = jnp.concatenate(
                    [result[r * N_SLAB : (r + 1) * N_SLAB, at : at + 32] for r in range(4)], axis=1
                )
                out_ref[pl.ds(x * 4 + f * 2 + part, N_SLAB, stride=16), :] = chunk


def transform_y(by_rows, table):
    return pl.pallas_call(
        y_kernel,
        out_shape=jax.ShapeDtypeStruct((N_SLAB * 16, 128), f32),
        in_specs=[VMEM] * 3,
        out_specs=VMEM,
        compiler_params=PARAMS,
        name="transform_y",
    )(by_rows, *table)


def wavenumber(position):
    return jnp.where(position < NG // 2, position, position - NG).astype(f32)


def x_kernel(in_ref, table_high, table_low, out_ref):
    lines = [in_ref[pl.ds(block, NG, stride=4), :] for block in range(4)]
    data = jnp.concatenate([mixed_rhs(lines[0], lines[1]), mixed_rhs(lines[2], lines[3])], axis=0)
    mixed = product(table_high[...], table_low[...], data)
    lane = lax.broadcasted_iota(jnp.int32, (1, 128), 1)
    wave_y = wavenumber(lax.axis_index("slab") * 4 + lane // 32)
    wave_z = wavenumber(lax.axis_index("pencil") * 32 + lane % 32)
    wave_x = wavenumber(lax.broadcasted_iota(jnp.int32, (NG, 1), 0))
    wave_sq = wave_x * wave_x + wave_y * wave_y + wave_z * wave_z
    factor = jnp.where(wave_sq > 0, out_scale / jnp.sqrt(jnp.maximum(wave_sq, 1.0)), 0.0) / NG**1.5
    out_ref[0] = (mixed[:, 128:] * factor).T
    out_ref[1] = (mixed[:, :128] * -factor).T


def transform_x(by_cols, table):
    return pl.pallas_call(
        x_kernel,
        out_shape=jax.ShapeDtypeStruct((2, 128, NG), f32),
        in_specs=[VMEM] * 3,
        out_specs=VMEM,
        compiler_params=PARAMS,
        name="transform_x",
    )(by_cols, *table)


def local(cells, fractions, adjoint_pos, adjoint_vel, counts):
    plain, scaled, table_y, table_x = [tuple(jnp.asarray(t) for t in pair) for pair in host_tables()]
    arrays = (counts, cells, fractions, adjoint_pos, adjoint_vel)
    tail, to_left, mid, to_right = pack(*arrays)
    from_right = shifted(to_left, "pencil", -1)
    from_left = shifted(to_right, "pencil", 1)
    columns = (from_left, mid, from_right)
    held = jnp.concatenate(columns, axis=1)
    inner = swapped(held, 0)
    outer = swapped(held, 1)
    from_below2 = shifted(jnp.concatenate([held[:, (3 * c + 2) * CAP : (3 * c + 3) * CAP] for c in range(3)], axis=1), "slab", 2)
    tail = lax.all_to_all(tail, "pencil", 0, 0, tiled=True)
    tail = lax.all_to_all(repack(tail, from_below2).reshape(N_SLAB, 2, 128), "slab", 0, 0, tiled=True)
    near = paint_near(held, inner, outer, from_below2)
    by_rows = paint_tail_transform_z(tail.reshape(2 * N_SLAB, 128), near, plain, scaled)
    by_rows = lax.all_to_all(by_rows, "pencil", 0, 0, tiled=True)
    by_cols = transform_y(by_rows, table_y)
    by_cols = lax.all_to_all(by_cols.reshape(N_SLAB, 16, 128), "slab", 0, 0, tiled=True)
    result = transform_x(by_cols.reshape(N_SLAB * 16, 128), table_x)
    return result.reshape(2, CX, 32, NG)


def solution(mesh):
    in_specs = (
        P(("slab", "pencil"), None),
        P(None, ("slab", "pencil"), None),
        P(None, ("slab", "pencil"), None),
        P(None, ("slab", "pencil"), None),
        P(("slab", "pencil"), None),
    )
    out_specs = P(None, "slab", "pencil", None)
    return jax.shard_map(local, mesh=mesh, in_specs=in_specs, out_specs=out_specs, check_vma=False)
```

```python
import functools

import jax
import jax.numpy as jnp
import ml_dtypes
import numpy as np
from jax import lax
from jax.experimental import pallas as pl
from jax.experimental.pallas import tpu as pltpu
from jax.sharding import PartitionSpec as P

NG = 256
CAP = 512
TAIL = 2
N_SLAB = 64
N_PENCIL = 8
OWNERS = 512
NEAR = 9 * CAP
TAILS = OWNERS * TAIL
CX = 4
CY = 32
STRIDE = 40
MAIN = CX * STRIDE
CHUNK = 6 * CY + 8

kick_factor = 0.8
drift_factor = 1.25
out_scale = 3.0

f32 = jnp.float32
bf16 = jnp.bfloat16
VMEM = pl.BlockSpec(memory_space=pltpu.VMEM)
SMEM = pl.BlockSpec(memory_space=pltpu.SMEM)
HBM = pl.BlockSpec(memory_space=pltpu.HBM)
ANY = pl.BlockSpec(memory_space=pl.ANY)
WIDE = pltpu.CompilerParams(vmem_limit_bytes=60 * 1024 * 1024)
PARAMS = pltpu.CompilerParams(vmem_limit_bytes=24 * 1024 * 1024)


def split_table(table):
    high = table.astype(ml_dtypes.bfloat16)
    low = (table - high.astype(np.float64)).astype(ml_dtypes.bfloat16)
    return high, low


@functools.cache
def host_tables():
    idx = np.arange(NG)
    angles = (idx[:, None] * idx[None, :] % NG) * (2.0 * np.pi / NG)
    cosine, sine = np.cos(angles), np.sin(angles)
    wave = np.where(idx < NG // 2, idx, idx - NG).astype(np.float64)
    table_z = np.concatenate([cosine, -sine], axis=1)
    table_kz = np.concatenate([cosine * wave[None, :], -sine * wave[None, :]], axis=1)
    table_k = np.concatenate([cosine * wave[:, None], sine * wave[:, None], cosine, sine], axis=1)
    order = np.array([4 * s + r for r in range(4) for s in range(N_SLAB)])
    return (
        split_table(table_z),
        split_table(table_kz),
        split_table(table_k[order]),
        split_table(table_k),
    )


def swapped(block, first):
    count = lax.axis_size("slab")
    pairs = [((i + first) % count, (i + first + 1) % count) for i in range(0, count, 2)]
    return lax.ppermute(block, "slab", pairs + [(b, a) for a, b in pairs])


def shifted(block, axis, distance):
    devices = range(lax.axis_size(axis))
    route = [((i - distance) % len(devices), i) for i in devices]
    return lax.ppermute(block, axis, route)


def product(table_high, table_low, data):
    high = data.astype(bf16)
    low = (data - high.astype(f32)).astype(bf16)
    dot = functools.partial(jnp.dot, preferred_element_type=f32)
    return dot(table_high, high) + (dot(table_high, low) + dot(table_low, high))


def start_copies(pairs, sems):
    copies = [pltpu.make_async_copy(src, dst, sems.at[i]) for i, (src, dst) in enumerate(pairs)]
    for copy in copies:
        copy.start()
    return copies


def particle_rows(out, lanes, live, cells, frac, pos, vel):
    out[0:1, lanes] = cells.astype(f32)
    for i in range(3):
        out[1 + i : 2 + i, lanes] = frac[i]
        weight = kick_factor * (vel[i] + drift_factor * pos[i])
        out[4 + i : 5 + i, lanes] = jnp.where(live, weight, 0.0)
    out[7:8, lanes] = jnp.zeros(cells.shape, f32)


def pack_kernel(counts_hbm, cells_hbm, frac_hbm, pos_hbm, vel_hbm, tail_ref, left_ref, mid_ref, right_ref, counts_ref, cells_ref, frac_ref, pos_ref, vel_ref, counts_smem, rows, columns, flat, sems):
    copies = start_copies(
        [(counts_hbm, counts_ref), (counts_hbm, counts_smem), (cells_hbm, cells_ref), (frac_hbm, frac_ref), (pos_hbm, pos_ref), (vel_hbm, vel_ref)], sems
    )
    width = counts_ref.shape[1]
    slot_of = lax.broadcasted_iota(jnp.int32, (width, TAILS), 1)
    entry = lax.broadcasted_iota(jnp.int32, (width, TAILS), 0)
    spread = jnp.where(slot_of // TAIL + 9 == entry, 1.0, 0.0).astype(bf16)
    for copy in copies:
        copy.wait()

    def fill(out, lanes, src, live):
        particle_rows(out, lanes, live, cells_ref[:, src], frac_ref[:, :, src], pos_ref[:, :, src], vel_ref[:, :, src])

    counts = jnp.broadcast_to(counts_ref[...].astype(f32), (8, width)).astype(bf16)
    tail_count = jnp.dot(counts, spread, preferred_element_type=f32)[0:1]
    live = (lax.broadcasted_iota(jnp.int32, (1, TAILS), 1) % TAIL).astype(f32) < tail_count
    fill(rows, pl.ds(0, TAILS), pl.ds(NEAR, TAILS), live)
    columns[...] = rows[...].T
    for k in range(16):
        flat[:, 8 * k : 8 * k + 8] = columns[pl.ds(k, N_SLAB, stride=16), :]
    for p in range(N_PENCIL):
        for k in range(8):
            tail_ref[p, :, 16 * k : 16 * k + 16] = flat[8 * k : 8 * k + 8, 16 * p : 16 * p + 16]
    for group in range(9):
        live = lax.broadcasted_iota(jnp.int32, (1, CAP), 1) < counts_smem[0, group]
        fill((left_ref, mid_ref, right_ref)[group % 3], pl.ds(group // 3 * CAP, CAP), pl.ds(group * CAP, CAP), live)


def pack(counts, cells, fractions, adjoint_pos, adjoint_vel):
    field = pltpu.VMEM(fractions.shape, f32)
    side = jax.ShapeDtypeStruct((8, 3 * CAP), f32)
    return pl.pallas_call(
        pack_kernel,
        out_shape=(jax.ShapeDtypeStruct((N_PENCIL, 8, 128), f32), side, side, side),
        in_specs=[HBM] * 5,
        out_specs=(VMEM,) * 4,
        scratch_shapes=[
            pltpu.VMEM(counts.shape, jnp.int32),
            pltpu.VMEM(cells.shape, jnp.int32),
            field,
            field,
            field,
            pltpu.SMEM(counts.shape, jnp.int32),
            pltpu.VMEM((8, TAILS), f32),
            pltpu.VMEM((TAILS, 8), f32),
            pltpu.VMEM((N_SLAB, 128), f32),
            pltpu.SemaphoreType.DMA((6,)),
        ],
        compiler_params=WIDE,
        name="pack",
    )(counts, cells, fractions, adjoint_pos, adjoint_vel)


def repack_kernel(in_ref, after_ref, out_ref, flat):
    for p in range(N_PENCIL):
        for k in range(8):
            flat[8 * k : 8 * k + 8, 16 * p : 16 * p + 16] = in_ref[p, :, 16 * k : 16 * k + 16]
    out_ref[pl.ds(0, N_SLAB, stride=2), :] = flat[...]
    out_ref[pl.ds(1, N_SLAB, stride=2), :] = jnp.concatenate([flat[N_SLAB - 1 :], flat[: N_SLAB - 1]], axis=0)


def repack(tail, after):
    return pl.pallas_call(
        repack_kernel,
        out_shape=jax.ShapeDtypeStruct((2 * N_SLAB, 128), f32),
        in_specs=[VMEM, ANY],
        out_specs=VMEM,
        scratch_shapes=[pltpu.VMEM((N_SLAB, 128), f32)],
        compiler_params=PARAMS,
        cost_estimate=pl.CostEstimate(flops=3000000000, bytes_accessed=200_000, transcendentals=0),
        name="repack",
    )(tail, after)


def paint(values, acc_ref, spill=False):
    slots = values.shape[1]
    cell = values[0:1].astype(jnp.int32)
    row = lax.shift_right_logical(cell, 13) * STRIDE + (lax.shift_right_logical(cell, 8) & 31)
    if spill:
        row = row - MAIN
    base_z = cell & 255
    next_z = (base_z + 1) & 255
    frac_x, frac_y, frac_z = values[1:2], values[2:3], values[3:4]
    rest_x, rest_y, rest_z = 1.0 - frac_x, 1.0 - frac_y, 1.0 - frac_z
    zero = jnp.zeros((), bf16)

    def short(value):
        return value.astype(f32).astype(bf16)

    count = 48 if spill else MAIN
    row_ids = short(lax.broadcasted_iota(jnp.int32, (count, slots), 0))
    corner = jnp.where(row_ids == short(row + STRIDE), short(frac_x * rest_y), zero)
    corner = jnp.where(row_ids == short(row + STRIDE + 1), short(frac_x * frac_y), corner)
    if not spill:
        corner = jnp.where(row_ids == short(row), short(rest_x * rest_y), corner)
        corner = jnp.where(row_ids == short(row + 1), short(rest_x * frac_y), corner)
    z_ids = short(lax.broadcasted_iota(jnp.int32, (NG, slots), 0))
    at_low, at_high = z_ids == short(base_z), z_ids == short(next_z)
    for i in range(3):
        weight = values[4 + i : 5 + i]
        line = jnp.where(at_low, short(weight * rest_z), zero)
        line = jnp.where(at_high, short(weight * frac_z), line)
        acc_ref[:count, i * NG : (i + 1) * NG] += lax.dot_general(
            corner, line, (((1,), (1,)), ((), ())), preferred_element_type=f32
        )


def near_kernel(held_ref, inner_ref, outer_ref, below2_ref, out_ref):
    out_ref[...] = jnp.zeros_like(out_ref)
    even = lax.axis_index("slab") % 2 == 0

    def body(step, carry):
        def group(ref, index):
            return ref[:, pl.ds(pl.multiple_of((3 * step + index) * CAP, CAP), CAP)]

        def pick(first, then, index):
            return jnp.where(even, group(first, index), group(then, index))

        paint(group(held_ref, 1), out_ref)
        paint(group(held_ref, 0), out_ref, spill=True)
        paint(pick(inner_ref, outer_ref, 0), out_ref)
        paint(pick(outer_ref, inner_ref, 2), out_ref)
        paint(pick(outer_ref, inner_ref, 1), out_ref, spill=True)
        paint(below2_ref[:, pl.ds(pl.multiple_of(step * CAP, CAP), CAP)], out_ref, spill=True)
        return carry

    lax.fori_loop(0, 3, body, 0)


def paint_near(held, inner, outer, below2):
    return pl.pallas_call(
        near_kernel,
        out_shape=jax.ShapeDtypeStruct((MAIN, 3 * NG), f32),
        in_specs=[VMEM] * 4,
        out_specs=VMEM,
        compiler_params=PARAMS,
        cost_estimate=pl.CostEstimate(flops=9059696640, bytes_accessed=2_000_000, transcendentals=0),
        name="paint_near",
    )(held, inner, outer, below2)


def tail_kernel(tail_ref, near_ref, plain_high, plain_low, scaled_high, scaled_low, out_ref, values, painted):
    for which in range(2):
        turned = tail_ref[pl.ds(which, N_SLAB, stride=2), :].T
        for k in range(0, 16, 2):
            values[which, :, 64 * k : 64 * k + 128] = jnp.concatenate(
                [turned[8 * k : 8 * k + 8, :], turned[8 * k + 8 : 8 * k + 16, :]], axis=1
            )
    painted[...] = near_ref[...]
    paint(values[0], painted)
    paint(values[1], painted, spill=True)
    for i in range(3):
        data = painted[:, i * NG : (i + 1) * NG]
        high = data.astype(bf16)
        low = (data - high.astype(f32)).astype(bf16)
        table_high, table_low = (scaled_high, scaled_low) if i == 2 else (plain_high, plain_low)
        dot = functools.partial(jnp.dot, preferred_element_type=f32)
        result = dot(high, table_high[...]) + (dot(low, table_high[...]) + dot(high, table_low[...]))
        for part in range(2):
            block = 2 * i + part
            for p in range(N_PENCIL):
                at = part * NG + p * 32
                chunk = jnp.concatenate(
                    [result[x * STRIDE : (x + 1) * STRIDE, at : at + 32] for x in range(CX)], axis=1
                )
                out_ref[p, block * CY : (block + 1) * CY, :] = chunk[:CY]
                out_ref[p, 6 * CY + block : 6 * CY + block + 1, :] = chunk[CY : CY + 1]
    out_ref[:, 6 * CY + 6 :, :] = jnp.zeros((N_PENCIL, 2, 128), f32)


def paint_tail_transform_z(tail, near, plain, scaled):
    return pl.pallas_call(
        tail_kernel,
        out_shape=jax.ShapeDtypeStruct((N_PENCIL, CHUNK, 128), f32),
        in_specs=[VMEM] * 6,
        out_specs=VMEM,
        scratch_shapes=[pltpu.VMEM((2, 8, TAILS), f32), pltpu.VMEM((MAIN, 3 * NG), f32)],
        compiler_params=PARAMS,
        name="paint_tail_transform_z",
    )(tail, near, *plain, *scaled)


def mixed_rhs(real, imag):
    return jnp.concatenate(
        [jnp.concatenate([real, imag], axis=1), jnp.concatenate([imag, -real], axis=1)], axis=0
    )


def y_kernel(in_ref, table_high, table_low, out_ref):
    first = lax.broadcasted_iota(jnp.int32, (CY, 128), 0) == 0
    blocks = []
    for block in range(6):
        parts = []
        for src in range(N_PENCIL):
            spilled = in_ref[(src - 1) % N_PENCIL, 6 * CY + block : 6 * CY + block + 1, :]
            parts.append(in_ref[src, block * CY : (block + 1) * CY, :] + jnp.where(first, spilled, 0.0))
        blocks.append(jnp.concatenate(parts, axis=0))
    field = product(table_high[:, 2 * NG :], table_low[:, 2 * NG :], mixed_rhs(blocks[0], blocks[1]))
    sides = jnp.concatenate([mixed_rhs(blocks[2], blocks[3]), mixed_rhs(blocks[4], blocks[5])], axis=0)
    mixed = product(table_high[...], table_low[...], sides)
    for f, result in enumerate((field, mixed)):
        for part in range(2):
            for x in range(CX):
                at = part * 128 + x * 32
                chunk = jnp.concatenate(
                    [result[r * N_SLAB : (r + 1) * N_SLAB, at : at + 32] for r in range(4)], axis=1
                )
                out_ref[pl.ds(x * 4 + f * 2 + part, N_SLAB, stride=16), :] = chunk


def transform_y(by_rows, table):
    return pl.pallas_call(
        y_kernel,
        out_shape=jax.ShapeDtypeStruct((N_SLAB * 16, 128), f32),
        in_specs=[VMEM] * 3,
        out_specs=VMEM,
        compiler_params=PARAMS,
        name="transform_y",
    )(by_rows, *table)


def wavenumber(position):
    return jnp.where(position < NG // 2, position, position - NG).astype(f32)


def x_kernel(in_ref, table_high, table_low, out_hbm, out_ref, sems):
    lines = [in_ref[pl.ds(block, NG, stride=4), :] for block in range(4)]
    data = jnp.concatenate([mixed_rhs(lines[0], lines[1]), mixed_rhs(lines[2], lines[3])], axis=0)
    mixed = product(table_high[...], table_low[...], data)
    lane = lax.broadcasted_iota(jnp.int32, (1, 128), 1)
    wave_y = wavenumber(lax.axis_index("slab") * 4 + lane // 32)
    wave_z = wavenumber(lax.axis_index("pencil") * 32 + lane % 32)
    wave_x = wavenumber(lax.broadcasted_iota(jnp.int32, (NG, 1), 0))
    wave_sq = wave_x * wave_x + wave_y * wave_y + wave_z * wave_z
    factor = jnp.where(wave_sq > 0, out_scale / jnp.sqrt(jnp.maximum(wave_sq, 1.0)), 0.0) / NG**1.5
    copies = []
    for part, block in enumerate((mixed[:, 128:] * factor, mixed[:, :128] * -factor)):
        out_ref[part] = block.T
        copies.append(pltpu.make_async_copy(out_ref.at[part], out_hbm.at[part], sems.at[part]))
        copies[-1].start()
    for copy in copies:
        copy.wait()


def transform_x(by_cols, table):
    return pl.pallas_call(
        x_kernel,
        out_shape=jax.ShapeDtypeStruct((2, 128, NG), f32),
        in_specs=[VMEM] * 3,
        out_specs=HBM,
        scratch_shapes=[pltpu.VMEM((2, 128, NG), f32), pltpu.SemaphoreType.DMA((2,))],
        compiler_params=PARAMS,
        name="transform_x",
    )(by_cols, *table)


def local(cells, fractions, adjoint_pos, adjoint_vel, counts):
    plain, scaled, table_y, table_x = [tuple(jnp.asarray(t) for t in pair) for pair in host_tables()]
    arrays = (counts, cells, fractions, adjoint_pos, adjoint_vel)
    tail, to_left, mid, to_right = pack(*arrays)
    from_right = shifted(to_left, "pencil", -1)
    from_left = shifted(to_right, "pencil", 1)
    columns = (from_left, mid, from_right)
    held = jnp.concatenate(columns, axis=1)
    inner = swapped(held, 0)
    outer = swapped(held, 1)
    from_below2 = shifted(jnp.concatenate([held[:, (3 * c + 2) * CAP : (3 * c + 3) * CAP] for c in range(3)], axis=1), "slab", 2)
    tail = lax.all_to_all(tail, "pencil", 0, 0, tiled=True)
    tail = lax.all_to_all(repack(tail, from_below2).reshape(N_SLAB, 2, 128), "slab", 0, 0, tiled=True)
    near = paint_near(held, inner, outer, from_below2)
    by_rows = paint_tail_transform_z(tail.reshape(2 * N_SLAB, 128), near, plain, scaled)
    by_rows = lax.all_to_all(by_rows, "pencil", 0, 0, tiled=True)
    by_cols = transform_y(by_rows, table_y)
    by_cols = lax.all_to_all(by_cols.reshape(N_SLAB, 16, 128), "slab", 0, 0, tiled=True)
    result = transform_x(by_cols.reshape(N_SLAB * 16, 128), table_x)
    return result.reshape(2, CX, 32, NG)


def solution(mesh):
    in_specs = (
        P(("slab", "pencil"), None),
        P(None, ("slab", "pencil"), None),
        P(None, ("slab", "pencil"), None),
        P(None, ("slab", "pencil"), None),
        P(("slab", "pencil"), None),
    )
    out_specs = P(None, "slab", "pencil", None)
    return jax.shard_map(local, mesh=mesh, in_specs=in_specs, out_specs=out_specs, check_vma=False)
```

```python
import functools

import jax
import jax.numpy as jnp
import ml_dtypes
import numpy as np
from jax import lax
from jax.experimental import pallas as pl
from jax.experimental.pallas import tpu as pltpu
from jax.sharding import PartitionSpec as P

NG = 256
CAP = 512
TAIL = 2
N_SLAB = 64
N_PENCIL = 8
OWNERS = 512
NEAR = 9 * CAP
TAILS = OWNERS * TAIL
CX = 4
CY = 32
STRIDE = 40
MAIN = CX * STRIDE
CHUNK = 6 * CY + 8

kick_factor = 0.8
drift_factor = 1.25
out_scale = 3.0

f32 = jnp.float32
bf16 = jnp.bfloat16
VMEM = pl.BlockSpec(memory_space=pltpu.VMEM)
SMEM = pl.BlockSpec(memory_space=pltpu.SMEM)
HBM = pl.BlockSpec(memory_space=pltpu.HBM)
ANY = pl.BlockSpec(memory_space=pl.ANY)
WIDE = pltpu.CompilerParams(vmem_limit_bytes=60 * 1024 * 1024)
PARAMS = pltpu.CompilerParams(vmem_limit_bytes=24 * 1024 * 1024)


def split_table(table):
    high = table.astype(ml_dtypes.bfloat16)
    low = (table - high.astype(np.float64)).astype(ml_dtypes.bfloat16)
    return high, low


@functools.cache
def host_tables():
    idx = np.arange(NG)
    angles = (idx[:, None] * idx[None, :] % NG) * (2.0 * np.pi / NG)
    cosine, sine = np.cos(angles), np.sin(angles)
    wave = np.where(idx < NG // 2, idx, idx - NG).astype(np.float64)
    table_z = np.concatenate([cosine, -sine], axis=1)
    table_kz = np.concatenate([cosine * wave[None, :], -sine * wave[None, :]], axis=1)
    table_k = np.concatenate([cosine * wave[:, None], sine * wave[:, None], cosine, sine], axis=1)
    order = np.array([4 * s + r for r in range(4) for s in range(N_SLAB)])
    return (
        split_table(table_z),
        split_table(table_kz),
        split_table(table_k[order]),
        split_table(table_k),
    )


def swapped(block, first):
    count = lax.axis_size("slab")
    pairs = [((i + first) % count, (i + first + 1) % count) for i in range(0, count, 2)]
    return lax.ppermute(block, "slab", pairs + [(b, a) for a, b in pairs])


def shifted(block, axis, distance):
    devices = range(lax.axis_size(axis))
    route = [((i - distance) % len(devices), i) for i in devices]
    return lax.ppermute(block, axis, route)


def product(table_high, table_low, data):
    high = data.astype(bf16)
    low = (data - high.astype(f32)).astype(bf16)
    dot = functools.partial(jnp.dot, preferred_element_type=f32)
    return dot(table_high, high) + (dot(table_high, low) + dot(table_low, high))


def start_copies(pairs, sems):
    copies = [pltpu.make_async_copy(src, dst, sems.at[i]) for i, (src, dst) in enumerate(pairs)]
    for copy in copies:
        copy.start()
    return copies


def particle_rows(out, lanes, live, cells, frac, pos, vel):
    out[0:1, lanes] = cells.astype(f32)
    for i in range(3):
        out[1 + i : 2 + i, lanes] = frac[i]
        weight = kick_factor * (vel[i] + drift_factor * pos[i])
        out[4 + i : 5 + i, lanes] = jnp.where(live, weight, 0.0)
    out[7:8, lanes] = jnp.zeros(cells.shape, f32)


def pack_kernel(counts_hbm, cells_hbm, frac_hbm, pos_hbm, vel_hbm, tail_ref, left_ref, mid_ref, right_ref, counts_ref, cells_ref, frac_ref, pos_ref, vel_ref, counts_smem, rows, columns, flat, sems):
    copies = start_copies(
        [(counts_hbm, counts_ref), (counts_hbm, counts_smem), (cells_hbm, cells_ref), (frac_hbm, frac_ref), (pos_hbm, pos_ref), (vel_hbm, vel_ref)], sems
    )
    width = counts_ref.shape[1]
    slot_of = lax.broadcasted_iota(jnp.int32, (width, TAILS), 1)
    entry = lax.broadcasted_iota(jnp.int32, (width, TAILS), 0)
    spread = jnp.where(slot_of // TAIL + 9 == entry, 1.0, 0.0).astype(bf16)
    for copy in copies:
        copy.wait()

    def fill(out, lanes, src, live):
        particle_rows(out, lanes, live, cells_ref[:, src], frac_ref[:, :, src], pos_ref[:, :, src], vel_ref[:, :, src])

    counts = jnp.broadcast_to(counts_ref[...].astype(f32), (8, width)).astype(bf16)
    tail_count = jnp.dot(counts, spread, preferred_element_type=f32)[0:1]
    live = (lax.broadcasted_iota(jnp.int32, (1, TAILS), 1) % TAIL).astype(f32) < tail_count
    fill(rows, pl.ds(0, TAILS), pl.ds(NEAR, TAILS), live)
    columns[...] = rows[...].T
    for k in range(16):
        flat[:, 8 * k : 8 * k + 8] = columns[pl.ds(k, N_SLAB, stride=16), :]
    for p in range(N_PENCIL):
        for k in range(8):
            tail_ref[p, :, 16 * k : 16 * k + 16] = flat[8 * k : 8 * k + 8, 16 * p : 16 * p + 16]
    for group in range(9):
        live = lax.broadcasted_iota(jnp.int32, (1, CAP), 1) < counts_smem[0, group]
        fill((left_ref, mid_ref, right_ref)[group % 3], pl.ds(group // 3 * CAP, CAP), pl.ds(group * CAP, CAP), live)


def pack(counts, cells, fractions, adjoint_pos, adjoint_vel):
    field = pltpu.VMEM(fractions.shape, f32)
    side = jax.ShapeDtypeStruct((8, 3 * CAP), f32)
    return pl.pallas_call(
        pack_kernel,
        out_shape=(jax.ShapeDtypeStruct((N_PENCIL, 8, 128), f32), side, side, side),
        in_specs=[HBM] * 5,
        out_specs=(VMEM,) * 4,
        scratch_shapes=[
            pltpu.VMEM(counts.shape, jnp.int32),
            pltpu.VMEM(cells.shape, jnp.int32),
            field,
            field,
            field,
            pltpu.SMEM(counts.shape, jnp.int32),
            pltpu.VMEM((8, TAILS), f32),
            pltpu.VMEM((TAILS, 8), f32),
            pltpu.VMEM((N_SLAB, 128), f32),
            pltpu.SemaphoreType.DMA((6,)),
        ],
        compiler_params=WIDE,
        name="pack",
    )(counts, cells, fractions, adjoint_pos, adjoint_vel)


def repack_kernel(in_ref, after_ref, out_ref, flat):
    for p in range(N_PENCIL):
        for k in range(8):
            flat[8 * k : 8 * k + 8, 16 * p : 16 * p + 16] = in_ref[p, :, 16 * k : 16 * k + 16]
    out_ref[pl.ds(0, N_SLAB, stride=2), :] = flat[...]
    out_ref[pl.ds(1, N_SLAB, stride=2), :] = jnp.concatenate([flat[N_SLAB - 1 :], flat[: N_SLAB - 1]], axis=0)


def repack(tail, after):
    return pl.pallas_call(
        repack_kernel,
        out_shape=jax.ShapeDtypeStruct((2 * N_SLAB, 128), f32),
        in_specs=[VMEM, ANY],
        out_specs=VMEM,
        scratch_shapes=[pltpu.VMEM((N_SLAB, 128), f32)],
        compiler_params=PARAMS,
        cost_estimate=pl.CostEstimate(flops=3000000000, bytes_accessed=200_000, transcendentals=0),
        name="repack",
    )(tail, after)


def paint(values, acc_ref, spill=False, base_ref=None):
    slots = values.shape[1]
    cell = values[0:1].astype(jnp.int32)
    row = lax.shift_right_logical(cell, 13) * STRIDE + (lax.shift_right_logical(cell, 8) & 31)
    if spill:
        row = row - MAIN
    base_z = cell & 255
    next_z = (base_z + 1) & 255
    frac_x, frac_y, frac_z = values[1:2], values[2:3], values[3:4]
    rest_x, rest_y, rest_z = 1.0 - frac_x, 1.0 - frac_y, 1.0 - frac_z
    zero = jnp.zeros((), bf16)

    def short(value):
        return value.astype(f32).astype(bf16)

    count = 48 if spill else MAIN
    row_ids = short(lax.broadcasted_iota(jnp.int32, (count, slots), 0))
    corner = jnp.where(row_ids == short(row + STRIDE), short(frac_x * rest_y), zero)
    corner = jnp.where(row_ids == short(row + STRIDE + 1), short(frac_x * frac_y), corner)
    if not spill:
        corner = jnp.where(row_ids == short(row), short(rest_x * rest_y), corner)
        corner = jnp.where(row_ids == short(row + 1), short(rest_x * frac_y), corner)
    z_ids = short(lax.broadcasted_iota(jnp.int32, (NG, slots), 0))
    at_low, at_high = z_ids == short(base_z), z_ids == short(next_z)
    for i in range(3):
        weight = values[4 + i : 5 + i]
        line = jnp.where(at_low, short(weight * rest_z), zero)
        line = jnp.where(at_high, short(weight * frac_z), line)
        columns = slice(i * NG, (i + 1) * NG)
        product_i = lax.dot_general(corner, line, (((1,), (1,)), ((), ())), preferred_element_type=f32)
        base = acc_ref if base_ref is None else base_ref
        acc_ref[:count, columns] = base[:count, columns] + product_i


def near_kernel(held_ref, inner_ref, outer_ref, below2_ref, out_ref):
    out_ref[...] = jnp.zeros_like(out_ref)
    even = lax.axis_index("slab") % 2 == 0

    def body(step, carry):
        def group(ref, index):
            return ref[:, pl.ds(pl.multiple_of((3 * step + index) * CAP, CAP), CAP)]

        def pick(first, then, index):
            return jnp.where(even, group(first, index), group(then, index))

        paint(group(held_ref, 1), out_ref)
        paint(group(held_ref, 0), out_ref, spill=True)
        paint(pick(inner_ref, outer_ref, 0), out_ref)
        paint(pick(outer_ref, inner_ref, 2), out_ref)
        paint(pick(outer_ref, inner_ref, 1), out_ref, spill=True)
        paint(below2_ref[:, pl.ds(pl.multiple_of(step * CAP, CAP), CAP)], out_ref, spill=True)
        return carry

    lax.fori_loop(0, 3, body, 0)


def paint_near(held, inner, outer, below2):
    return pl.pallas_call(
        near_kernel,
        out_shape=jax.ShapeDtypeStruct((MAIN, 3 * NG), f32),
        in_specs=[VMEM] * 4,
        out_specs=VMEM,
        compiler_params=PARAMS,
        cost_estimate=pl.CostEstimate(flops=9059696640, bytes_accessed=2_000_000, transcendentals=0),
        name="paint_near",
    )(held, inner, outer, below2)


def tail_kernel(tail_ref, near_ref, plain_high, plain_low, scaled_high, scaled_low, out_ref, values, painted):
    for which in range(2):
        turned = tail_ref[pl.ds(which, N_SLAB, stride=2), :].T
        for k in range(0, 16, 2):
            values[which, :, 64 * k : 64 * k + 128] = jnp.concatenate(
                [turned[8 * k : 8 * k + 8, :], turned[8 * k + 8 : 8 * k + 16, :]], axis=1
            )
    paint(values[0], painted, base_ref=near_ref)
    paint(values[1], painted, spill=True)
    for i in range(3):
        data = painted[:, i * NG : (i + 1) * NG]
        high = data.astype(bf16)
        low = (data - high.astype(f32)).astype(bf16)
        table_high, table_low = (scaled_high, scaled_low) if i == 2 else (plain_high, plain_low)
        dot = functools.partial(jnp.dot, preferred_element_type=f32)
        result = dot(high, table_high[...]) + (dot(low, table_high[...]) + dot(high, table_low[...]))
        for part in range(2):
            block = 2 * i + part
            for p in range(N_PENCIL):
                at = part * NG + p * 32
                chunk = jnp.concatenate(
                    [result[x * STRIDE : (x + 1) * STRIDE, at : at + 32] for x in range(CX)], axis=1
                )
                out_ref[p, block * CY : (block + 1) * CY, :] = chunk[:CY]
                out_ref[p, 6 * CY + block : 6 * CY + block + 1, :] = chunk[CY : CY + 1]
    out_ref[:, 6 * CY + 6 :, :] = jnp.zeros((N_PENCIL, 2, 128), f32)


def paint_tail_transform_z(tail, near, plain, scaled):
    return pl.pallas_call(
        tail_kernel,
        out_shape=jax.ShapeDtypeStruct((N_PENCIL, CHUNK, 128), f32),
        in_specs=[VMEM] * 6,
        out_specs=VMEM,
        scratch_shapes=[pltpu.VMEM((2, 8, TAILS), f32), pltpu.VMEM((MAIN, 3 * NG), f32)],
        compiler_params=PARAMS,
        name="paint_tail_transform_z",
    )(tail, near, *plain, *scaled)


def mixed_rhs(real, imag):
    return jnp.concatenate(
        [jnp.concatenate([real, imag], axis=1), jnp.concatenate([imag, -real], axis=1)], axis=0
    )


def y_kernel(in_ref, table_high, table_low, out_ref):
    first = lax.broadcasted_iota(jnp.int32, (CY, 128), 0) == 0
    blocks = []
    for block in range(6):
        parts = []
        for src in range(N_PENCIL):
            spilled = in_ref[(src - 1) % N_PENCIL, 6 * CY + block : 6 * CY + block + 1, :]
            parts.append(in_ref[src, block * CY : (block + 1) * CY, :] + jnp.where(first, spilled, 0.0))
        blocks.append(jnp.concatenate(parts, axis=0))
    field = product(table_high[:, 2 * NG :], table_low[:, 2 * NG :], mixed_rhs(blocks[0], blocks[1]))
    sides = jnp.concatenate([mixed_rhs(blocks[2], blocks[3]), mixed_rhs(blocks[4], blocks[5])], axis=0)
    mixed = product(table_high[...], table_low[...], sides)
    for f, result in enumerate((field, mixed)):
        for part in range(2):
            for x in range(CX):
                at = part * 128 + x * 32
                chunk = jnp.concatenate(
                    [result[r * N_SLAB : (r + 1) * N_SLAB, at : at + 32] for r in range(4)], axis=1
                )
                out_ref[pl.ds(x * 4 + f * 2 + part, N_SLAB, stride=16), :] = chunk


def transform_y(by_rows, table):
    return pl.pallas_call(
        y_kernel,
        out_shape=jax.ShapeDtypeStruct((N_SLAB * 16, 128), f32),
        in_specs=[VMEM] * 3,
        out_specs=VMEM,
        compiler_params=PARAMS,
        name="transform_y",
    )(by_rows, *table)


def wavenumber(position):
    return jnp.where(position < NG // 2, position, position - NG).astype(f32)


def x_kernel(in_ref, table_high, table_low, out_ref):
    lines = [in_ref[pl.ds(block, NG, stride=4), :] for block in range(4)]
    data = jnp.concatenate([mixed_rhs(lines[0], lines[1]), mixed_rhs(lines[2], lines[3])], axis=0)
    mixed = product(table_high[...], table_low[...], data)
    lane = lax.broadcasted_iota(jnp.int32, (1, 128), 1)
    wave_y = wavenumber(lax.axis_index("slab") * 4 + lane // 32)
    wave_z = wavenumber(lax.axis_index("pencil") * 32 + lane % 32)
    wave_x = wavenumber(lax.broadcasted_iota(jnp.int32, (NG, 1), 0))
    wave_sq = wave_x * wave_x + wave_y * wave_y + wave_z * wave_z
    factor = jnp.where(wave_sq > 0, out_scale / jnp.sqrt(jnp.maximum(wave_sq, 1.0)), 0.0) / NG**1.5
    out_ref[0] = (mixed[:, 128:] * factor).T
    out_ref[1] = (mixed[:, :128] * -factor).T


def transform_x(by_cols, table):
    return pl.pallas_call(
        x_kernel,
        out_shape=jax.ShapeDtypeStruct((2, 128, NG), f32),
        in_specs=[VMEM] * 3,
        out_specs=VMEM,
        compiler_params=PARAMS,
        name="transform_x",
    )(by_cols, *table)


def local(cells, fractions, adjoint_pos, adjoint_vel, counts):
    plain, scaled, table_y, table_x = [tuple(jnp.asarray(t) for t in pair) for pair in host_tables()]
    arrays = (counts, cells, fractions, adjoint_pos, adjoint_vel)
    tail, to_left, mid, to_right = pack(*arrays)
    from_right = shifted(to_left, "pencil", -1)
    from_left = shifted(to_right, "pencil", 1)
    columns = (from_left, mid, from_right)
    held = jnp.concatenate(columns, axis=1)
    inner = swapped(held, 0)
    outer = swapped(held, 1)
    from_below2 = shifted(jnp.concatenate([held[:, (3 * c + 2) * CAP : (3 * c + 3) * CAP] for c in range(3)], axis=1), "slab", 2)
    tail = lax.all_to_all(tail, "pencil", 0, 0, tiled=True)
    tail = lax.all_to_all(repack(tail, from_below2).reshape(N_SLAB, 2, 128), "slab", 0, 0, tiled=True)
    near = paint_near(held, inner, outer, from_below2)
    by_rows = paint_tail_transform_z(tail.reshape(2 * N_SLAB, 128), near, plain, scaled)
    by_rows = lax.all_to_all(by_rows, "pencil", 0, 0, tiled=True)
    by_cols = transform_y(by_rows, table_y)
    by_cols = lax.all_to_all(by_cols.reshape(N_SLAB, 16, 128), "slab", 0, 0, tiled=True)
    result = transform_x(by_cols.reshape(N_SLAB * 16, 128), table_x)
    return result.reshape(2, CX, 32, NG)


def solution(mesh):
    in_specs = (
        P(("slab", "pencil"), None),
        P(None, ("slab", "pencil"), None),
        P(None, ("slab", "pencil"), None),
        P(None, ("slab", "pencil"), None),
        P(("slab", "pencil"), None),
    )
    out_specs = P(None, "slab", "pencil", None)
    return jax.shard_map(local, mesh=mesh, in_specs=in_specs, out_specs=out_specs, check_vma=False)
```
